256 devices in a mesh: section: 4 (over x), feat: 32 (over z, y), row: 2 (over core).
Axes of the slice: x: 4, y: 4, z: 8, core: 2. Of those that a mesh axis runs over, the one named last changes fastest.
Arguments:
- target_ids: int32 [8], replicated, may hold values from 0 to 16383
- target_pos: int32 [8], replicated, may hold values from 0 to 31
- target_gain: float32 [4608], replicated, may hold values from 0.1 to 1.9
- target_scale: float32 [32], replicated, may hold values from 0.3 to 3
- encoder: bfloat16 [16384, 4608], P(('feat', 'row')), may hold values from -6 to 6
- post_gain: float32 [4, 4608], P('section'), may hold values from 0.1 to 1.9
- post_scale: float32 [4, 32], P('section'), may hold values from 0.3 to 3
- out_proj: bfloat16 [4, 32, 128, 4608], P('section', 'feat'), may hold values from -0.09375 to 0.09375
- pattern: bfloat16 [4, 32, 32, 32], P('section', 'feat'), may hold values from 0 to 1, as said below
- value_proj: bfloat16 [4, 32, 4608, 128], P('section', 'feat'), may hold values from -0.1875 to 0.1875
- pre_gain: float32 [4, 4608], P('section'), may hold values from 0.1 to 1.9
- pre_scale: float32 [4, 32], P('section'), may hold values from 0.3 to 3
- decoder: bfloat16 [4, 2, 8192, 4608], P('section', None, 'feat'), may hold values from -0.09375 to 0.09375
- block_ids: int32 [4, 512, 128], P('section', 'feat'), may hold values from 0 to 255
- block_pos: int32 [4, 512], P('section', 'feat'), may hold values from 0 to 31
- block_act: float32 [4, 512, 128], P('section', 'feat'), may hold values from 0 to 4, as said below
- block_count: int32 [4, 32], P('section', 'feat'), may hold values from 1 to 16, as said below
Outputs:
- attributions: float32 [4, 8, 512, 128], P('section', 'row', 'feat')
- gradients: bfloat16 [4, 8, 32, 4608], P('section', 'row', None, 'feat')
The draws below stay inside these ranges and needn't reach their ends.
Inputs may be any that keep to these rules, and one draw needn't show every extreme that they name: Each head's pattern is zero above the diagonal and its rows sum to one up to rounding. `block_act`: rows of activation 0 in a live block are padding. Owner o's blocks of layer l are the slots o * 16 to o * 16 + block_count[l, o] - 1; later slots hold entries without meaning. In every layer some owner has exactly 16 live blocks.
All inputs are finite; a program needn't handle non-finite values.
Results may differ from the reference program's by a relative error of at most 0.035.
Values may be sent and summed in bfloat16 or wider, within the bound.
A program may use at most 128 MiB of HBM per device.

```python
import math
import jax
import jax.numpy as jnp
from jax import lax

D = 4608
HD = 128
HEAD_DEV = 1
SEQ = 32
DICT_DEV = 256
BLOCK_DEV = 16
BLOCK_ROWS = 128
LAYERS = 4
HEADS = 32
OWNERS = 32
TARGETS = 8
BLOCKS = 512
DEC_ROWS = 8192
ENC_ROWS = 16384


def draw_pattern(key, part):
    key = jax.random.fold_in(key, 11)
    raw_weights = jnp.exp(1.5 * jax.random.normal(key, (LAYERS, HEADS, SEQ, SEQ), jnp.float32))
    causal = jnp.arange(SEQ)[:, None] >= jnp.arange(SEQ)[None, :]
    weights = jnp.where(causal, raw_weights, 0.0)
    return (weights / jnp.sum(weights, axis=-1, keepdims=True)).astype(jnp.bfloat16)


def draw_block_act(key, part):
    key = jax.random.fold_in(key, 12)
    live_key, value_key = jax.random.split(key)
    act_shape = (LAYERS, BLOCKS, BLOCK_ROWS)
    live_rows = jax.random.uniform(live_key, act_shape, jnp.float32) < 0.8
    values = jnp.exp(jax.random.uniform(value_key, act_shape, jnp.float32, math.log(0.1), math.log(4.0)))
    return jnp.where(live_rows, values, 0.0)


def draw_block_count(key, part):
    key = jax.random.fold_in(key, 13)
    base_key, full_key = jax.random.split(key)
    counts = jax.random.randint(base_key, (LAYERS, OWNERS), 1, BLOCK_DEV // 2 + 1)
    fullest = jax.random.randint(full_key, (LAYERS, 1), 0, OWNERS)
    return jnp.where(jnp.arange(OWNERS)[None, :] == fullest, BLOCK_DEV, counts).astype(jnp.int32)


def set_ends(values, stream_key, smallest, largest):
    spot = [jax.random.randint(jax.random.fold_in(stream_key, axis), (), 0, length) for axis, length in enumerate(values.shape)]
    main_axis = values.shape.index(max(values.shape))
    beside = spot[:main_axis] + [(spot[main_axis] + 1) % values.shape[main_axis]] + spot[main_axis + 1:]
    return values.at[tuple(spot)].set(smallest).at[tuple(beside)].set(largest)


def strengthened(entries, stream_key, source, target, shards_of, factor):
    owner, partner = [(jnp.arange(entries.shape[axis_at]) // (entries.shape[axis_at] // shards_of)).reshape([-1 if axis == axis_at else 1 for axis in range(entries.ndim)]) for axis_at in (source, target)]
    chosen = jax.random.permutation(stream_key, shards_of)[partner]
    strong = (owner == chosen) | (owner == (partner + shards_of // 2) % shards_of)
    return jnp.where(strong, factor * entries, entries)


def block_scale(key, shape, shards, least, high):
    level, own = 1.0, jax.random.fold_in(key, 6)
    for dim, parts in shards:
        steps = jnp.exp(jax.random.uniform(jax.random.fold_in(own, dim), (parts,), jnp.float32, least / len(shards), high / len(shards)))
        level = level * jnp.repeat(steps, shape[dim] // parts).reshape([-1 if axis == dim else 1 for axis in range(len(shape))])
    return level


def centred(key, extent, scale, reach, cuts=(), kind=jnp.bfloat16):
    level = block_scale(key, extent, cuts, -0.22, 0.18) if cuts else 1.0
    values = jax.random.normal(key, extent, jnp.float32) * scale * level
    return jnp.minimum(jnp.maximum(values, -reach), reach).astype(kind)


def gaussian_with(own_key, shape, deviation, reach, cuts, heavy, kind=jnp.bfloat16):
    entries = deviation * jax.random.normal(own_key, shape, jnp.float32)
    if cuts:
        entries = entries * block_scale(own_key, shape, cuts, -0.22, 0.18)
    return jnp.clip(strengthened(entries, jax.random.fold_in(own_key, 3), *heavy), -reach, reach).astype(kind)


def setup_inputs(seed: int = 0) -> dict:
    splits = jax.random.split(jax.random.key(seed), 18)
    return {
        "target_ids": set_ends(jax.random.randint(splits[0], (TARGETS,), 0, ENC_ROWS), jax.random.fold_in(splits[0], 1), 0, ENC_ROWS - 1).astype(jnp.int32),
        "target_pos": set_ends(jax.random.randint(splits[1], (TARGETS,), 0, SEQ), jax.random.fold_in(splits[1], 1), 0, SEQ - 1).astype(jnp.int32),
        "target_gain": jnp.clip(1.0 + 0.18 * jax.random.normal(splits[2], (D,), jnp.float32), 0.1, 1.9),
        "target_scale": jnp.clip(jnp.exp(jax.random.uniform(splits[3], (SEQ,), jnp.float32, math.log(0.3), math.log(3.0))), 0.3, 3.0),
        "encoder": centred(splits[4], (ENC_ROWS, D), 1.0, 6.0, ((0, 64),)),
        "post_gain": jnp.clip(1.0 + 0.18 * jax.random.normal(splits[5], (LAYERS, D), jnp.float32), 0.1, 1.9),
        "post_scale": jnp.clip(jnp.exp(math.log(3.0) - 2.3025851 * jax.random.uniform(splits[6], (LAYERS, SEQ), jnp.float32) ** block_scale(splits[6], (LAYERS, SEQ), ((0, 4),), -0.2, 0.2)), 0.3, 3.0),
        "out_proj": centred(splits[7], (LAYERS, HEADS, HD, D), D ** -0.5, 0.09375, ((0, 4), (1, 32))),
        "pattern": draw_pattern(jax.random.fold_in(splits[17], 71), 0),
        "value_proj": gaussian_with(splits[9], (LAYERS, HEADS, D, HD), (HD * HEADS) ** -0.5, 0.1875, ((0, 4), (1, 32)), (1, 2, 32, 2.75)),
        "pre_gain": jnp.clip(1.0 + 0.18 * jax.random.normal(splits[10], (LAYERS, D), jnp.float32), 0.1, 1.9),
        "pre_scale": jnp.clip(jnp.exp(math.log(3.0) - 2.3025851 * jax.random.uniform(splits[11], (LAYERS, SEQ), jnp.float32) ** block_scale(splits[11], (LAYERS, SEQ), ((0, 4),), -0.2, 0.2)), 0.3, 3.0),
        "decoder": centred(splits[12], (LAYERS, 2, DEC_ROWS, D), D ** -0.5, 0.09375, ((0, 4), (2, 32))),
        "block_ids": set_ends(jax.random.randint(splits[13], (LAYERS, BLOCKS, BLOCK_ROWS), 0, DICT_DEV), jax.random.fold_in(splits[13], 1), 0, DICT_DEV - 1).astype(jnp.int32),
        "block_pos": set_ends(jax.random.randint(splits[14], (LAYERS, BLOCKS), 0, SEQ), jax.random.fold_in(splits[14], 1), 0, SEQ - 1).astype(jnp.int32),
        "block_act": draw_block_act(jax.random.fold_in(splits[17], 71), 0),
        "block_count": draw_block_count(jax.random.fold_in(splits[17], 71), 0),
    }


def back_layer(grad_above, post_gain_row, post_scale_row, out_weights, mix_weights, value_weights, pre_gain_row, pre_scale_row):
    scaled = (grad_above.astype(jnp.float32) * post_gain_row[None, None, :] * post_scale_row[None, :, None]).astype(jnp.bfloat16)
    head_in = jnp.einsum('tsd,hed->tshe', scaled.astype(jnp.float32), out_weights.astype(jnp.float32)).astype(jnp.bfloat16)
    head_mix = jnp.einsum('hqp,tqhe->tphe', mix_weights.astype(jnp.float32), head_in.astype(jnp.float32)).astype(jnp.bfloat16)
    grouped = head_mix.reshape(TARGETS, SEQ, OWNERS, HEAD_DEV, HD).transpose(2, 0, 1, 3, 4)
    weight_groups = value_weights.reshape(OWNERS, HEAD_DEV, D, HD)

    def add_group(running, pieces):
        mixed_part, weight_part = pieces
        head_part = jnp.einsum('tphe,hde->tpd', mixed_part.astype(jnp.float32), weight_part.astype(jnp.float32))
        head_part = head_part * pre_gain_row[None, None, :] * pre_scale_row[None, :, None]
        rounded = lax.optimization_barrier(head_part.astype(jnp.bfloat16))
        return running + rounded.astype(jnp.float32), None

    summed, unused = lax.scan(add_group, jnp.zeros((TARGETS, SEQ, D), jnp.float32), (grouped, weight_groups))
    return (grad_above.astype(jnp.float32) + summed).astype(jnp.bfloat16)


def layer_scores(grad_out, grad_in, dec_layer, ids_layer, pos_layer, act_layer, count_layer):
    ids_own = ids_layer.reshape(OWNERS, BLOCK_DEV, BLOCK_ROWS)
    pos_own = pos_layer.reshape(OWNERS, BLOCK_DEV)
    act_own = act_layer.reshape(OWNERS, BLOCK_DEV, BLOCK_ROWS)
    owners_all = jnp.arange(OWNERS, dtype=jnp.int32)

    def per_owner(pieces):
        owner_num, owner_ids, owner_pos, owner_act, owner_count = pieces
        start_row = (owner_num * DICT_DEV).astype(jnp.int32)
        dec_write = lax.dynamic_slice_in_dim(dec_layer[0], start_row, DICT_DEV, 0).astype(jnp.float32)
        dec_next = lax.dynamic_slice_in_dim(dec_layer[1], start_row, DICT_DEV, 0).astype(jnp.float32)
        rows_out = jnp.take(grad_out, owner_pos, axis=1).astype(jnp.float32)
        rows_in = jnp.take(grad_in, owner_pos, axis=1).astype(jnp.float32)
        scores = jnp.einsum('tbd,fd->tbf', rows_out, dec_write) + jnp.einsum('tbd,fd->tbf', rows_in, dec_next)
        index_all = jnp.broadcast_to(owner_ids[None], (TARGETS, BLOCK_DEV, BLOCK_ROWS))
        picked = jnp.take_along_axis(scores, index_all, axis=2)
        live_blocks = jnp.arange(BLOCK_DEV, dtype=jnp.int32) < owner_count
        return jnp.where(live_blocks[None, :, None], picked * owner_act[None], jnp.zeros_like(picked))

    result = lax.map(per_owner, (owners_all, ids_own, pos_own, act_own, count_layer))
    return result.transpose(1, 0, 2, 3).reshape(TARGETS, BLOCKS, BLOCK_ROWS)


def reference(target_ids, target_pos, target_gain, target_scale, encoder, post_gain, post_scale, out_proj, pattern, value_proj, pre_gain, pre_scale, decoder, block_ids, block_pos, block_act, block_count):
    target_rows = jnp.take(encoder, target_ids, axis=0).astype(jnp.float32) * target_gain[None, :]
    hit_scale = (jnp.arange(SEQ, dtype=jnp.int32)[None, :] == target_pos[:, None]).astype(jnp.float32) * target_scale[None, :]
    grad_now = (hit_scale[:, :, None] * target_rows[:, None, :]).astype(jnp.bfloat16)
    grads_list = [None] * LAYERS
    scores_list = [None] * LAYERS
    for layer_num in reversed(range(LAYERS)):
        grad_below = back_layer(grad_now, post_gain[layer_num], post_scale[layer_num], out_proj[layer_num], pattern[layer_num], value_proj[layer_num], pre_gain[layer_num], pre_scale[layer_num])
        scores_list[layer_num] = layer_scores(grad_below, grad_now, decoder[layer_num], block_ids[layer_num], block_pos[layer_num], block_act[layer_num], block_count[layer_num])
        grads_list[layer_num] = grad_below
        grad_now = grad_below
    return jnp.stack(scores_list), jnp.stack(grads_list)
```

```python
import functools

import jax
import jax.numpy as jnp
from jax import lax
from jax.experimental import pallas as pl
from jax.experimental.pallas import tpu as pltpu
from jax.sharding import PartitionSpec as P

MESH = pl.DeviceIdType.MESH
F32 = jnp.float32
BF16 = jnp.bfloat16
NT = (((1,), (1,)), ((), ()))
TN = (((0,), (0,)), ((), ()))

D, HD, SEQ, FEATS, TGT = 4608, 128, 32, 32, 4
NZ, NY = 8, 4
SL = D // FEATS
COLS = TGT * SEQ
QUARTER = D // NY
PIECE = 640
STEP = QUARTER - PIECE
Z_ORDER = (1, 7, 2, 6, 3, 5, 4)
Y_ORDER = (1, 3, 2)


def main_kernel(
    ids_ref, pos_ref, tgain_ref, tscale_ref, pgain_ref, pscale_ref, qgain_ref, qscale_ref, pattern_ref,
    enc_hbm, out_hbm, val_hbm, dec_hbm,
    score_ref, grad_ref,
    enc, outp, val, dec, rows, e1, e2, e3, e2src, msg, recv, gslice, qslice,
    vt, full_in, full_mix, full_out,
    load_sem, e_send, e_recv, p_send, p_recv, v_send, v_recv, g_send, g_recv, x_send, x_recv,
):
    s = lax.axis_index("section")
    f = lax.axis_index("feat")
    c = lax.axis_index("row")
    z = f // NY
    y = f % NY

    def zdev(dz):
        return (s, lax.rem(z + dz, NZ) * NY + y, c)

    def ydev(dy):
        return (s, z * NY + lax.rem(y + dy, NY), c)

    def fdev(k):
        return (s, lax.rem(f + k, FEATS), c)

    def ycdev(k):
        j = lax.rem(y * 2 + c + k, 8)
        return (s, z * NY + j // 2, j % 2)

    def remote(src, dst, ss, rs, dev):
        return pltpu.make_async_remote_copy(
            src_ref=src, dst_ref=dst, send_sem=ss, recv_sem=rs, device_id=dev, device_id_type=MESH
        )

    load_enc = pltpu.make_async_copy(enc_hbm, enc, load_sem.at[0])
    load_out = pltpu.make_async_copy(out_hbm.at[0, 0], outp, load_sem.at[1])
    load_val = pltpu.make_async_copy(val_hbm.at[0, 0], val, load_sem.at[2])
    load_dec = pltpu.make_async_copy(dec_hbm.at[0], dec, load_sem.at[3])

    barrier = pltpu.get_barrier_semaphore()

    def greet(k, carry):
        pl.semaphore_signal(barrier, inc=1, device_id=fdev(k), device_id_type=MESH)
        return carry

    lax.fori_loop(1, FEATS, greet, 0)

    @pl.when(s == 3)
    def _():
        load_enc.start()

        def greet_cross(k, carry):
            j = lax.rem(y + k, NY)
            pl.semaphore_signal(barrier, inc=1, device_id=(s, z * NY + j, 1 - c), device_id_type=MESH)
            return carry

        lax.fori_loop(0, NY, greet_cross, 0)

    @pl.when(s < 3)
    def _():
        pl.semaphore_signal(barrier, inc=1, device_id=(s + 1, f, c), device_id_type=MESH)

    load_out.start()
    load_val.start()
    load_dec.start()

    lane_t = lax.broadcasted_iota(jnp.int32, (8, COLS), 1) // SEQ
    lane_p = lax.broadcasted_iota(jnp.int32, (8, COLS), 1) % SEQ
    row_t = lax.broadcasted_iota(jnp.int32, (8, COLS), 0)

    pattern4 = jnp.concatenate([pattern_ref[0, 0].astype(F32)] * TGT, axis=1)
    pscale4 = jnp.concatenate([pscale_ref[...]] * TGT, axis=1)
    qscale4 = jnp.concatenate([qscale_ref[...]] * TGT, axis=1)

    def column_of(gain_ref):
        for k in range(FEATS):
            qslice[k] = gain_ref[:, k * SL:(k + 1) * SL]
        row = qslice[f]
        eye = lax.broadcasted_iota(jnp.int32, (SL, SL), 0) == lax.broadcasted_iota(jnp.int32, (SL, SL), 1)
        return jnp.sum(jnp.where(eye, jnp.broadcast_to(row, (SL, SL)), 0.0), axis=1, keepdims=True)

    def gather_start(full, blk, k):
        def copy(b, dev, i):
            part = full.at[pl.ds(pl.multiple_of(b * blk, 16), blk)]
            return remote(part, part, g_send.at[k, i], g_recv.at[k, b], dev)

        sent = []
        for i, dy in enumerate(Y_ORDER):
            sent.append(copy(f, ydev(dy), i))
            sent[-1].start()
        for i, dz in enumerate(Z_ORDER):
            sent.append(copy(f, zdev(dz), 3 + i))
            sent[-1].start()
        for i, dz in enumerate(Z_ORDER):
            b = lax.rem(z + NZ - dz, NZ) * NY + y
            copy(b, zdev(0), 3 + i).wait_recv()
            for j, dy in enumerate(Y_ORDER):
                sent.append(copy(b, ydev(dy), 10 + 3 * i + j))
                sent[-1].start()
        return sent, copy

    def gather(full, blk, k):
        sent, copy = gather_start(full, blk, k)
        for dz in (0,) + Z_ORDER:
            for dy in Y_ORDER:
                b = lax.rem(z + NZ - dz, NZ) * NY + lax.rem(y + dy, NY)
                copy(b, ydev(1), 0).wait_recv()
        return sent

    def finish(sent):
        for item in sent:
            item.wait_send()

    own = pl.ds(pl.multiple_of(f * SL, 16), SL)
    own_head = pl.ds(pl.multiple_of(f * HD, 128), HD)

    def pass_down(block_src):
        return remote(block_src, full_in.at[own], x_send, x_recv, (lax.rem(s + 3, 4), f, c))

    @pl.when(s == 3)
    def _():
        load_enc.wait()
        base = (f * 2 + c) * enc.shape[0]
        wanted = jnp.full((8, 1), -1, jnp.int32)
        for t in range(8):
            wanted = jnp.where(lax.broadcasted_iota(jnp.int32, (8, 1), 0) == t, ids_ref[t] - base, wanted)
        hit = lax.broadcasted_iota(jnp.int32, (8, enc.shape[0]), 1) == wanted
        rows[...] = jnp.dot(hit.astype(BF16), enc[...], preferred_element_type=F32)

        pl.semaphore_wait(barrier, FEATS + NY)

        me = y * 2 + c

        def e_copy(stage, src, dst, k, slot, dev):
            return remote(src, dst.at[slot], e_send.at[stage, k], e_recv.at[stage, slot], dev)

        def piece_of(j):
            return rows.at[:, pl.ds(pl.multiple_of((j // 2) * QUARTER + (j % 2) * STEP, 128), PIECE)]

        def e1_copy(k):
            return e_copy(0, piece_of(lax.rem(me + k, 8)), e1, k, me, ycdev(k))

        for k in range(1, 8):
            e1_copy(k).start()
        e1[me] = piece_of(me)[...]
        for k in range(1, 8):
            j = lax.rem(me + k, 8)
            e_copy(0, e2src, e1, 0, j, ycdev(1)).wait_recv()
        total = e1[0]
        for k in range(1, 8):
            total = total + e1[k]
        e2src[...] = total

        def e2_copy(dz):
            return e_copy(1, e2src, e2, dz, z, zdev(dz))

        for dz in Z_ORDER:
            e2_copy(dz).start()
        e2[z] = total
        for dz in Z_ORDER:
            e_copy(1, e2src, e2, 0, lax.rem(z + dz, NZ), zdev(1)).wait_recv()
        total = e2[0]
        for k in range(1, 8):
            total = total + e2[k]
        e3[me] = total

        def e3_copy(k):
            return e_copy(2, e3.at[me], e3, k, me, ycdev(k))

        for k in range(1, 8):
            e3_copy(k).start()
        for k in range(1, 8):
            j = lax.rem(me + k, 8)
            e_copy(2, e2src, e3, 0, j, ycdev(1)).wait_recv()
        pieces = []
        for k in range(NY):
            pieces.append(e3[2 * k])
            pieces.append(e3[2 * k + 1][:, PIECE - STEP:])
        raw = jnp.concatenate(pieces, axis=1)
        raw = jnp.where(c == 0, raw, pltpu.roll(raw, 4, 0))
        own_row = lax.broadcasted_iota(jnp.int32, (8, 1), 0)
        raw = jnp.where(own_row < TGT, raw, 0.0)

        at = jnp.full((8, 1), -1, jnp.int32)
        for t in range(TGT):
            at = jnp.where(own_row == t, jnp.where(c == 0, pos_ref[t], pos_ref[t + TGT]), at)
        at_pos = lax.broadcasted_iota(jnp.int32, (8, SEQ), 1) == at
        t_scale = jnp.sum(jnp.where(at_pos, jnp.broadcast_to(tscale_ref[...], (8, SEQ)), 0.0), axis=1, keepdims=True)
        p_scale = jnp.sum(jnp.where(at_pos, jnp.broadcast_to(pscale_ref[...], (8, SEQ)), 0.0), axis=1, keepdims=True)
        top = (raw * tgain_ref[...] * t_scale).astype(BF16)
        scaled = (top.astype(F32) * pgain_ref[...] * p_scale).astype(BF16)
        for k in range(1, 8):
            e1_copy(k).wait_send()
        rows[...] = top.astype(F32)
        load_out.wait()
        head_in = lax.dot_general(scaled, outp[...], NT, preferred_element_type=F32).astype(BF16)
        at_row = jnp.dot(at_pos.astype(BF16), pattern4.astype(BF16), preferred_element_type=F32)
        at_row = jnp.where(lane_t == row_t, at_row * qscale4, 0.0)
        load_val.wait()
        gap = jnp.zeros((SEQ - (SL - HD), HD), BF16)
        for k in range(FEATS):
            tail = val[k * SL + HD:(k + 1) * SL, :]
            weights = jnp.concatenate([val[k * SL:k * SL + HD, :]] + [tail, gap] * TGT, axis=0)
            out = lax.dot_general(head_in, weights, NT, preferred_element_type=F32)
            spread = jnp.where(lane_t == (row_t + 1) % TGT, out[:, HD:], 0.0)
            low = pltpu.roll(spread + at_row, 4, 0)
            msg[k] = jnp.where(row_t < TGT, out[:, :HD], low)

        def m_copy(k):
            return remote(msg.at[lax.rem(f + k, FEATS)], recv.at[f], p_send.at[k], p_recv.at[f], fdev(k))

        def m_start(k, carry):
            m_copy(k).start()
            return carry

        lax.fori_loop(1, FEATS, m_start, 0)
        recv[f] = msg[f]
        column = column_of(qgain_ref)
        for k in range(FEATS):
            gslice[k] = rows[:, k * SL:(k + 1) * SL]
        top_own = gslice[f].astype(BF16)
        at_lane = ((lane_t == row_t) & (lane_p == at)).astype(BF16)
        base_grad = lax.dot_general(top_own, at_lane, TN, preferred_element_type=F32)
        load_dec.wait()
        top_scores = lax.dot_general(dec[1], rows[...].astype(BF16), NT, preferred_element_type=F32)
        top_part = jnp.dot(top_scores, at_lane.astype(F32), preferred_element_type=F32,
                           precision=lax.Precision.HIGHEST)

        def m_wait(k, carry):
            j = lax.rem(f + k, FEATS)
            remote(msg.at[0], recv.at[j], p_send.at[0], p_recv.at[j], fdev(1)).wait_recv()
            return carry

        lax.fori_loop(1, FEATS, m_wait, 0)
        got = recv[...].reshape(FEATS * 8, COLS)
        got_row = lax.broadcasted_iota(jnp.int32, got.shape, 0) % 8
        got_t = lax.broadcasted_iota(jnp.int32, got.shape, 1) // SEQ
        low = jnp.where((got_row >= TGT) & (got_t == got_row - TGT), got, 0.0)
        high = pltpu.roll(low, FEATS * 8 - TGT, 0)
        left = got.astype(BF16)
        upper = lax.dot_general(left, high.astype(BF16), TN, preferred_element_type=F32)
        under = lax.dot_general(left, low.astype(BF16), TN, preferred_element_type=F32)
        tail_t = lax.broadcasted_iota(jnp.int32, (SL - HD, COLS), 1) // SEQ
        tail = jnp.zeros((SL - HD, COLS), F32)
        for t in range(TGT):
            start = SEQ * ((t + 1) % TGT)
            tail = tail + jnp.where(tail_t == t, under[start:start + SL - HD, :], 0.0)
        new = base_grad + jnp.concatenate([upper, tail], axis=0) * column
        grad_ref[...] = new.astype(BF16).astype(F32)
        full_out[own, :] = new.astype(BF16)
        down = pass_down(full_out.at[own])
        down.start()
        sent = gather(full_out, SL, 2)
        score_ref[...] = top_part + jnp.dot(dec[0], full_out[...], preferred_element_type=F32)
        for k in range(1, 8):
            e3_copy(k).wait_send()
        for dz in Z_ORDER:
            e2_copy(dz).wait_send()

        def m_done(k, carry):
            m_copy(k).wait_send()
            return carry

        lax.fori_loop(1, FEATS, m_done, 0)
        down.wait_send()
        finish(sent)

    @pl.when(s < 3)
    def _():
        @pl.when(s > 0)
        def _():
            pl.semaphore_wait(barrier, FEATS)

        @pl.when(s == 0)
        def _():
            pl.semaphore_wait(barrier, FEATS - 1)

        load_val.wait()

        def v_copy(k):
            j = lax.rem(f + k, FEATS)
            return remote(val.at[pl.ds(pl.multiple_of(j * SL, 16), SL)], vt.at[:, own_head],
                          v_send.at[k], v_recv.at[f], fdev(k))

        def v_start(k, carry):
            v_copy(k).start()
            return carry

        lax.fori_loop(1, FEATS, v_start, 0)
        vt[:, own_head] = val[own, :]
        column = column_of(qgain_ref)
        load_out.wait()
        outp[...] = (outp[...].astype(F32) * pgain_ref[...]).astype(BF16)
        mixer = jnp.concatenate([pattern4] * TGT, axis=0)
        mix_q = lax.broadcasted_iota(jnp.int32, mixer.shape, 0) // SEQ
        mix_p = lax.broadcasted_iota(jnp.int32, mixer.shape, 1) // SEQ
        mixer = jnp.where(mix_q == mix_p, mixer, 0.0).astype(BF16)
        load_dec.wait()

        def v_wait(k, carry):
            j = lax.rem(f + k, FEATS)
            part = pl.ds(pl.multiple_of(j * HD, 128), HD)
            remote(val.at[own], vt.at[:, part], v_send.at[0], v_recv.at[j], fdev(1)).wait_recv()
            return carry

        lax.fori_loop(1, FEATS, v_wait, 0)

        def v_done(k, carry):
            v_copy(k).wait_send()
            return carry

        lax.fori_loop(1, FEATS, v_done, 0)

        pass_down(full_out.at[own]).wait_recv()
        sent = gather(full_in, SL, 0)
        head_in = jnp.dot(outp[...], full_in[...], preferred_element_type=F32)
        head_in = (head_in * pscale4).astype(BF16)
        head_mix = jnp.dot(head_in, mixer, preferred_element_type=F32) * qscale4
        full_mix[own_head, :] = head_mix.astype(BF16)
        sent = sent + gather(full_mix, HD, 1)
        new = jnp.dot(vt[...], full_mix[...], preferred_element_type=F32) * column
        new = new + full_in[own, :].astype(F32)
        grad_ref[...] = new.astype(BF16).astype(F32)
        full_out[own, :] = new.astype(BF16)
        down = pass_down(full_out.at[own])

        @pl.when(s > 0)
        def _():
            down.start()

        part_scores = jnp.dot(dec[1], full_in[...], preferred_element_type=F32)
        score_ref[...] = part_scores
        sent = sent + gather(full_out, SL, 2)
        score_ref[...] += jnp.dot(dec[0], full_out[...], preferred_element_type=F32)

        @pl.when(s > 0)
        def _():
            down.wait_send()

        finish(sent)


def pick_kernel(pos_ref, count_ref, ids_ref, act_ref, score_ref, grad_ref, out_ref, grad_out_ref, turned, picked):
    turned[...] = score_ref[...].T
    grad_out_ref[0] = grad_ref[...].T.astype(BF16).reshape(TGT, SEQ, SL)
    slots, width = ids_ref.shape[1], ids_ref.shape[2]
    for b in range(slots):
        at = pos_ref[0, b]
        for t in range(TGT):
            picked[t, b:b + 1, :] = turned[pl.ds(t * SEQ + at, 1), :]
    ids = ids_ref[0]
    live = lax.broadcasted_iota(jnp.int32, (slots, width), 0) < count_ref[0, 0]
    inner = ids % 128
    for t in range(TGT):
        low = jnp.take_along_axis(picked[t, :, :128], inner, axis=1, mode="promise_in_bounds")
        high = jnp.take_along_axis(picked[t, :, 128:], inner, axis=1, mode="promise_in_bounds")
        value = jnp.where(ids < 128, low, high) * act_ref[0]
        out_ref[0, t] = jnp.where(live, value, 0.0)


def body(
    target_ids, target_pos, target_gain, target_scale, encoder, post_gain, post_scale, out_proj, pattern,
    value_proj, pre_gain, pre_scale, decoder, block_ids, block_pos, block_act, block_count,
):
    vmem = pl.BlockSpec(memory_space=pltpu.VMEM)
    smem = pl.BlockSpec(memory_space=pltpu.SMEM)
    hbm = pl.BlockSpec(memory_space=pl.ANY)
    dma = pltpu.SemaphoreType.DMA
    shard = encoder.shape[0]
    features = decoder.shape[2]
    scores, grads = pl.pallas_call(
        main_kernel,
        out_shape=(
            jax.ShapeDtypeStruct((features, COLS), F32),
            jax.ShapeDtypeStruct((SL, COLS), F32),
        ),
        in_specs=[smem, smem] + [vmem] * 7 + [hbm] * 4,
        out_specs=(vmem, vmem),
        scratch_shapes=[
            pltpu.VMEM((shard, D), BF16),
            pltpu.VMEM((HD, D), BF16),
            pltpu.VMEM((D, HD), BF16),
            pltpu.VMEM((2, features, D), BF16),
            pltpu.VMEM((8, D), F32),
            pltpu.VMEM((8, 8, PIECE), F32),
            pltpu.VMEM((8, 8, PIECE), F32),
            pltpu.VMEM((8, 8, PIECE), F32),
            pltpu.VMEM((8, PIECE), F32),
            pltpu.VMEM((FEATS, 8, COLS), F32),
            pltpu.VMEM((FEATS, 8, COLS), F32),
            pltpu.VMEM((FEATS, 8, SL), F32),
            pltpu.VMEM((FEATS, 1, SL), F32),
            pltpu.VMEM((SL, FEATS * HD), BF16),
            pltpu.VMEM((D, COLS), BF16),
            pltpu.VMEM((FEATS * HD, COLS), BF16),
            pltpu.VMEM((D, COLS), BF16),
            dma((4,)),
            dma((3, 8)),
            dma((3, 8)),
            dma((FEATS,)),
            dma((FEATS,)),
            dma((FEATS,)),
            dma((FEATS,)),
            dma((3, FEATS)),
            dma((3, FEATS)),
            dma,
            dma,
        ],
        compiler_params=pltpu.CompilerParams(
            collective_id=1, has_side_effects=True, vmem_limit_bytes=48 * 1024 * 1024
        ),
        name="chain",
    )(
        target_ids, target_pos, target_gain.reshape(1, D), target_scale.reshape(1, SEQ), post_gain, post_scale,
        pre_gain, pre_scale, pattern, encoder, out_proj, value_proj, decoder,
    )
    slots, width = block_ids.shape[1], block_ids.shape[2]
    return pl.pallas_call(
        pick_kernel,
        out_shape=(
            jax.ShapeDtypeStruct((1, TGT, slots, width), F32),
            jax.ShapeDtypeStruct((1, TGT, SEQ, SL), BF16),
        ),
        in_specs=[smem, smem] + [vmem] * 4,
        out_specs=(vmem, vmem),
        scratch_shapes=[pltpu.VMEM((COLS, features), F32), pltpu.VMEM((TGT, slots, features), F32)],
        name="pick",
    )(block_pos, block_count, block_ids, block_act, scores, grads)


def solution(mesh):
    in_specs = (
        P(),
        P(),
        P(),
        P(),
        P(("feat", "row"), None),
        P("section", None),
        P("section", None),
        P("section", "feat", None, None),
        P("section", "feat", None, None),
        P("section", "feat", None, None),
        P("section", None),
        P("section", None),
        P("section", None, "feat", None),
        P("section", "feat", None),
        P("section", "feat"),
        P("section", "feat", None),
        P("section", "feat"),
    )
    out_specs = (P("section", "row", "feat", None), P("section", "row", None, "feat"))
    return jax.shard_map(body, mesh=mesh, in_specs=in_specs, out_specs=out_specs, check_vma=False)
```

```python
import functools

import jax
import jax.numpy as jnp
from jax import lax
from jax.experimental import pallas as pl
from jax.experimental.pallas import tpu as pltpu
from jax.sharding import PartitionSpec as P

MESH = pl.DeviceIdType.MESH
F32 = jnp.float32
BF16 = jnp.bfloat16
NT = (((1,), (1,)), ((), ()))
TN = (((0,), (0,)), ((), ()))

D, HD, SEQ, FEATS, TGT = 4608, 128, 32, 32, 4
NZ, NY = 8, 4
SL = D // FEATS
COLS = TGT * SEQ
QUARTER = D // NY
BLOCK = D // NZ
WIN = 640
PAD = WIN - BLOCK
Z_ORDER = (1, 7, 2, 6, 3, 5, 4)
Z_FAR = (4, 3, 5, 2, 6, 1, 7)
Y_ORDER = (1, 3, 2)
Y_FAR = (2, 1, 3)


def main_kernel(
    ids_hbm, pos_hbm, tgain_hbm, tscale_hbm, pgain_hbm, pscale_hbm, qgain_hbm, qscale_hbm, pattern_hbm,
    enc_hbm, out_hbm, val_hbm, dec_hbm,
    score_ref, grad_ref,
    ids_ref, pos_ref, tgain_ref, tscale_ref, pgain_ref, pscale_ref, qgain_ref, qscale_ref, pattern_ref,
    enc, outp, val, dec, rows, rows0, top_own, e1, e2, e3, e2src, msg, recv, gslice, qslice,
    ow, vw, mixw, gin, hsrc, hpart, hm, gsrc, gpart, res, up, out,
    load_sem, small_sem, core_sem, e_send, e_recv, p_send, p_recv, w_send, w_recv,
    gin_send, gin_recv, attr_send, h_send, h_recv, m_send, m_recv, y_send, y_recv, g_send, g_recv, go_sem,
):
    s = lax.axis_index("section")
    f = lax.axis_index("feat")
    c = lax.axis_index("row")
    z = f // NY
    y = f % NY

    def zdev(dz):
        return (s, lax.rem(z + dz, NZ) * NY + y, c)

    def ydev(dy):
        return (s, z * NY + lax.rem(y + dy, NY), c)

    def fdev(k):
        return (s, lax.rem(f + k, FEATS), c)

    def remote(src, dst, ss, rs, dev):
        return pltpu.make_async_remote_copy(
            src_ref=src, dst_ref=dst, send_sem=ss, recv_sem=rs, device_id=dev, device_id_type=MESH
        )

    load_enc = pltpu.make_async_copy(enc_hbm, enc, load_sem.at[0])
    load_out = pltpu.make_async_copy(out_hbm.at[0, 0], outp, load_sem.at[1])
    load_val = pltpu.make_async_copy(val_hbm.at[0, 0], val, load_sem.at[2])
    load_dec = pltpu.make_async_copy(dec_hbm.at[0], dec, load_sem.at[3])
    small = ((ids_hbm, ids_ref), (pos_hbm, pos_ref), (tgain_hbm, tgain_ref), (tscale_hbm, tscale_ref),
             (pgain_hbm, pgain_ref), (pscale_hbm, pscale_ref), (qgain_hbm, qgain_ref), (qscale_hbm, qscale_ref),
             (pattern_hbm, pattern_ref))
    small = [pltpu.make_async_copy(src, dst, small_sem.at[i]) for i, (src, dst) in enumerate(small)]

    @pl.when(s == 3)
    def _():
        load_enc.start()

    for item in small:
        item.start()
    load_out.start()
    load_val.start()
    load_dec.start()

    barrier = pltpu.get_barrier_semaphore()

    def hello(dev):
        pl.semaphore_signal(barrier, inc=1, device_id=dev, device_id_type=MESH)

    @pl.when(c == 0)
    def _():
        for dz in Z_ORDER:
            hello(zdev(dz))
        for dy in Y_ORDER:
            hello(ydev(dy))

    @pl.when(c == 1)
    def _():
        for dz in Z_ORDER:
            hello(zdev(dz))
        for dy in Y_ORDER:
            hello(ydev(dy))

        def other_planes(k, carry):
            q = lax.rem(s + k, 4)
            for dz in range(NZ):
                hello((q, lax.rem(z + dz, NZ) * NY + y, 1))
            for dy in Y_ORDER:
                hello((q, z * NY + lax.rem(y + dy, NY), 1))
            return carry

        lax.fori_loop(1, 4, other_planes, 0)

        @pl.when(s == 3)
        def _():
            def rest(dz, carry):
                for dy in Y_ORDER:
                    hello((s, lax.rem(z + dz, NZ) * NY + lax.rem(y + dy, NY), 1))
                return carry

            lax.fori_loop(1, NZ, rest, 0)

    for q in range(4):
        hello((q, f, 1 - c))
    for item in small:
        item.wait()

    lane_t = lax.broadcasted_iota(jnp.int32, (8, COLS), 1) // SEQ
    lane_p = lax.broadcasted_iota(jnp.int32, (8, COLS), 1) % SEQ
    row_t = lax.broadcasted_iota(jnp.int32, (8, COLS), 0)
    own_row = lax.broadcasted_iota(jnp.int32, (8, 1), 0)
    own = pl.ds(pl.multiple_of(f * SL, 16), SL)
    gin_own = pl.ds(pl.multiple_of(PAD + y * SL, 16), SL)
    pattern = pattern_ref[0, 0].astype(F32)

    def column(row):
        n = row.shape[1]
        eye = lax.broadcasted_iota(jnp.int32, (n, n), 0) == lax.broadcasted_iota(jnp.int32, (n, n), 1)
        return jnp.sum(jnp.where(eye, jnp.broadcast_to(row, (n, n)), 0.0), axis=1, keepdims=True)

    def pick_rows():
        load_enc.wait()
        base = (f * 2 + c) * enc.shape[0]
        wanted = jnp.full((8, 1), -1, jnp.int32)
        for t in range(8):
            wanted = jnp.where(own_row == t, ids_ref[t] - base, wanted)
        hit = lax.broadcasted_iota(jnp.int32, (8, enc.shape[0]), 1) == wanted
        rows[...] = jnp.dot(hit.astype(BF16), enc[...], preferred_element_type=F32)

    def positions(group):
        at = jnp.full((8, 1), -1, jnp.int32)
        for t in range(TGT):
            at = jnp.where(own_row == t, pos_ref[t + TGT * group], at)
        return at

    def top_scores(group):
        at_lane = ((lane_t == row_t) & (lane_p == positions(group))).astype(F32)
        part = lax.dot_general(dec[1], top_own[...].astype(BF16), NT, preferred_element_type=F32)
        score_ref[...] = jnp.dot(part, at_lane, preferred_element_type=F32, precision=lax.Precision.HIGHEST)

    def gather(full, k, sent, use, arrives=True):
        def copy(b, dev, i):
            part = full.at[pl.ds(pl.multiple_of(b * SL, 16), SL)]
            return remote(part, part, g_send.at[k, i], g_recv.at[k, b], dev)

        def start(item):
            item.start()
            sent.append(item)

        def forward(b, i):
            for j, dy in enumerate(Y_ORDER):
                start(copy(b, ydev(dy), 3 * i + j))

        if arrives:
            copy(f, ydev(1), 0).wait_recv()
        forward(f, 0)
        for i, dz in enumerate(Z_ORDER):
            start(copy(f, zdev(dz), 24 + i))
        for i, dz in enumerate(Z_ORDER):
            b = lax.rem(z + NZ - dz, NZ) * NY + y
            copy(b, ydev(1), 0).wait_recv()
            forward(b, 1 + i)
        span = 2 * NY * SL
        for dq in (0, 1, 3, 2):
            q = lax.rem(z // 2 + dq, NZ // 2)
            for half in range(2):
                for dy in Y_ORDER:
                    b = (2 * q + half) * NY + lax.rem(y + dy, NY)
                    copy(b, ydev(1), 0).wait_recv()
            part = pl.ds(pl.multiple_of(q * span, 128), span)
            use(part, full[part, :])

    def add_up(part, block):
        score_ref[...] += jnp.dot(dec[1, :, part], block, preferred_element_type=F32)

    def add_out(part, block):
        score_ref[...] += jnp.dot(dec[0, :, part], block, preferred_element_type=F32)

    def finish(sent):
        for item in sent:
            item.wait_send()

    def attribution_copy(src, full, k, layer, group, i):
        return remote(src, full.at[own], attr_send.at[i], g_recv.at[k, f], (layer, f, group))

    def gin_copy(src, plane, dy, i, j):
        dev = (plane, z * NY + lax.rem(y + dy, NY), 1)
        return remote(src, gin.at[i, gin_own], gin_send.at[j, dy], gin_recv.at[i, y], dev)

    def gin_wait(i, dy):
        j = lax.rem(y + dy, NY)
        part = gin.at[i, pl.ds(pl.multiple_of(PAD + j * SL, 16), SL)]
        remote(part, part, gin_send.at[0, 0], gin_recv.at[i, j], ydev(1)).wait_recv()

    def w_copies(dest, di, slot, dz, kind):
        zz = lax.rem(z + dz, NZ)
        dev = (dest, zz * NY + y, 1)
        ss, rs = w_send.at[di, kind, dz], w_recv.at[slot, kind, z]
        if kind == 0:
            first = pl.multiple_of(zz * BLOCK - PAD * (zz % 2), 128)
            return remote(outp.at[:, pl.ds(first, WIN)], ow.at[slot, z], ss, rs, dev)
        src = val.at[pl.ds(pl.multiple_of(zz * BLOCK, 16), BLOCK)]
        dst = vw.at[slot, :, pl.ds(pl.multiple_of(z * HD, 128), HD)]
        return remote(src, dst, ss, rs, dev)

    def mix_copy(dest, di, slot):
        return remote(mixw.at[2], mixw.at[slot], w_send.at[di, 2, 0], w_recv.at[slot, 2, 0], (dest, f, 1))

    dest0 = jnp.where(s == 1, 1, 2)
    dest1 = jnp.where(s == 1, 0, 3)
    w_slot = jnp.where(s == 0, 1, 0)

    def weights_start():
        load_out.wait()
        outp[...] = (outp[...].astype(F32) * pgain_ref[...]).astype(BF16)
        scaled = pattern * column(pscale_ref[...]) * qscale_ref[...]
        wide = jnp.concatenate([scaled] * TGT, axis=1)
        wide = jnp.concatenate([wide] * TGT, axis=0)
        same = (lax.broadcasted_iota(jnp.int32, wide.shape, 0) // SEQ
                == lax.broadcasted_iota(jnp.int32, wide.shape, 1) // SEQ)
        mixw[2] = jnp.where(same, wide, 0.0).astype(BF16)

        def both(kind):
            for dz in Z_FAR:
                w_copies(dest0, 0, w_slot, dz, kind).start()
                w_copies(dest1, 1, w_slot, dz, kind).start()
            w_copies(dest1, 1, w_slot, 0, kind).start()

            @pl.when(s == 0)
            def _():
                w_copies(dest0, 0, w_slot, 0, kind).start()

        both(0)
        mix_copy(dest1, 1, w_slot).start()

        @pl.when(s == 0)
        def _():
            mix_copy(dest0, 0, w_slot).start()

        @pl.when(s > 0)
        def _():
            mixw[0] = mixw[2]
            ow[0, z] = outp[:, pl.ds(pl.multiple_of(z * BLOCK - PAD * (z % 2), 128), WIN)]

        load_val.wait()
        for k in range(FEATS):
            part = slice(k * SL, (k + 1) * SL)
            val[part, :] = (val[part, :].astype(F32) * column(qgain_ref[:, part])).astype(BF16)
        both(1)

        @pl.when(s > 0)
        def _():
            vw[0, :, pl.ds(pl.multiple_of(z * HD, 128), HD)] = val[pl.ds(pl.multiple_of(z * BLOCK, 16), BLOCK), :]

    def weights_done():
        for kind in range(2):
            for dz in Z_FAR:
                w_copies(dest0, 0, w_slot, dz, kind).wait_send()
                w_copies(dest1, 1, w_slot, dz, kind).wait_send()
            w_copies(dest1, 1, w_slot, 0, kind).wait_send()

            @pl.when(s == 0)
            def _():
                w_copies(dest0, 0, w_slot, 0, kind).wait_send()

        mix_copy(dest1, 1, w_slot).wait_send()

        @pl.when(s == 0)
        def _():
            mix_copy(dest0, 0, w_slot).wait_send()

    def w_wait(i, kind, home):
        def one(dz):
            zz = lax.rem(z + dz, NZ)
            if kind == 0:
                part = ow.at[i, zz]
            else:
                part = vw.at[i, :, pl.ds(pl.multiple_of(zz * HD, 128), HD)]
            remote(part, part, w_send.at[0, 0, 0], w_recv.at[i, kind, zz], ydev(1)).wait_recv()

        for dz in Z_ORDER:
            one(dz)
        if i == 1:
            one(0)
        else:
            @pl.when(jnp.logical_not(home))
            def _():
                one(0)

    def m_wait(i, home):
        def one():
            remote(mixw.at[i], mixw.at[i], w_send.at[0, 0, 0], w_recv.at[i, 2, 0], ydev(1)).wait_recv()

        if i == 1:
            one()
        else:
            pl.when(jnp.logical_not(home))(one)

    def layer_step(i):
        home = (s == 1) | (s == 2)
        gin[i, 0:PAD] = jnp.zeros((PAD, COLS), BF16)
        gin[i, PAD + BLOCK:] = jnp.zeros((PAD, COLS), BF16)
        w_wait(i, 0, home)
        m_wait(i, home)
        for dy in Y_ORDER:
            gin_wait(i, dy)
        if i == 1:
            gin_wait(i, 0)
        else:
            @pl.when(s < 3)
            def _():
                gin_wait(i, 0)

        block = gin[i, pl.ds(pl.multiple_of(PAD * (1 - z % 2), 16), WIN), :]

        def h_copy(dz):
            zz = lax.rem(z + dz, NZ)
            return remote(hsrc.at[i, zz], hpart.at[i, z], h_send.at[i, dz], h_recv.at[i, z], zdev(dz))

        for dz in Z_FAR:
            zz = lax.rem(z + dz, NZ)
            hsrc[i, zz] = jnp.dot(ow[i, zz], block, preferred_element_type=F32).astype(BF16)
            h_copy(dz).start()
        total = jnp.dot(ow[i, z], block, preferred_element_type=F32)
        for dz in Z_ORDER:
            zz = lax.rem(z + dz, NZ)
            remote(hpart.at[i, zz], hpart.at[i, zz], h_send.at[i, 0], h_recv.at[i, zz], ydev(1)).wait_recv()
            total = total + hpart[i, zz].astype(F32)
        mixed = jnp.dot(total.astype(BF16), mixw[i], preferred_element_type=F32).astype(BF16)
        mine = pl.ds(pl.multiple_of(z * HD, 128), HD)
        hm[i, mine, :] = mixed

        def hm_copy(dz):
            return remote(hm.at[i, mine], hm.at[i, mine], m_send.at[i, dz], m_recv.at[i, z], zdev(dz))

        for dz in Z_FAR:
            hm_copy(dz).start()
        w_wait(i, 1, home)
        for dz in Z_ORDER:
            zz = lax.rem(z + dz, NZ)
            part = hm.at[i, pl.ds(pl.multiple_of(zz * HD, 128), HD)]
            remote(part, part, m_send.at[i, 0], m_recv.at[i, zz], ydev(1)).wait_recv()

        def g_part(dy):
            yy = lax.rem(y + dy, NY)
            weights = vw[i, pl.ds(pl.multiple_of(yy * SL, 16), SL), :]
            return jnp.dot(weights, hm[i], preferred_element_type=F32)

        def gp_copy(dy):
            yy = lax.rem(y + dy, NY)
            return remote(gsrc.at[i, yy], gpart.at[i, y], y_send.at[i, dy], y_recv.at[i, y], ydev(dy))

        for dy in Y_FAR:
            gsrc[i, lax.rem(y + dy, NY)] = g_part(dy).astype(BF16)
            gp_copy(dy).start()
        total = g_part(0) + gin[i, gin_own, :].astype(F32)
        for dy in Y_ORDER:
            yy = lax.rem(y + dy, NY)
            remote(gpart.at[i, yy], gpart.at[i, yy], y_send.at[i, 0], y_recv.at[i, yy], ydev(1)).wait_recv()
            total = total + gpart[i, yy].astype(F32)
        res[i] = total.astype(BF16)

        def done():
            for dz in Z_FAR:
                h_copy(dz).wait_send()
                hm_copy(dz).wait_send()
            for dy in Y_FAR:
                gp_copy(dy).wait_send()

        return done

    def top_layer():
        me = y

        def quarter(j):
            return rows.at[:, pl.ds(pl.multiple_of(j * QUARTER, 128), QUARTER)]

        def e_copy(stage, src, dst, k, slot, dev):
            return remote(src, dst.at[slot], e_send.at[stage, k], e_recv.at[stage, slot], dev)

        remote(rows0, rows0, core_sem.at[0], core_sem.at[1], (s, f, 0)).wait_recv()
        rows[...] = rows[...] + rows0[...]

        def e1_copy(dy):
            return e_copy(0, quarter(lax.rem(y + dy, NY)), e1, dy, me, ydev(dy))

        for dy in Y_FAR:
            e1_copy(dy).start()
        total = quarter(me)[...]
        for dy in Y_ORDER:
            j = lax.rem(y + dy, NY)
            e_copy(0, e2src, e1, 0, j, ydev(1)).wait_recv()
            total = total + e1[j]
        e2src[...] = total

        def e2_copy(dz):
            return e_copy(1, e2src, e2, dz, z, zdev(dz))

        for dz in Z_FAR:
            e2_copy(dz).start()
        for dz in Z_ORDER:
            j = lax.rem(z + dz, NZ)
            e_copy(1, e2src, e2, 0, j, ydev(1)).wait_recv()
            total = total + e2[j]
        e3[me] = total

        def e3_copy(dy):
            return e_copy(2, e3.at[me], e3, dy, me, ydev(dy))

        for dy in Y_FAR:
            e3_copy(dy).start()
        for dy in Y_ORDER:
            e_copy(2, e2src, e3, 0, lax.rem(y + dy, NY), ydev(1)).wait_recv()
        for dy in Y_FAR:
            e1_copy(dy).wait_send()
        raw = jnp.concatenate([e3[k] for k in range(NY)], axis=1)

        tops, scaled, at_rows, lanes = [], [], [], []
        pattern4 = jnp.concatenate([pattern] * TGT, axis=1)
        qscale4 = jnp.concatenate([qscale_ref[...]] * TGT, axis=1)
        for group in range(2):
            part = raw if group == 0 else pltpu.roll(raw, TGT, 0)
            part = jnp.where(own_row < TGT, part, 0.0)
            at = positions(group)
            at_pos = lax.broadcasted_iota(jnp.int32, (8, SEQ), 1) == at
            t_scale = jnp.sum(jnp.where(at_pos, jnp.broadcast_to(tscale_ref[...], (8, SEQ)), 0.0),
                              axis=1, keepdims=True)
            p_scale = jnp.sum(jnp.where(at_pos, jnp.broadcast_to(pscale_ref[...], (8, SEQ)), 0.0),
                              axis=1, keepdims=True)
            top = (part * tgain_ref[...] * t_scale).astype(BF16).astype(F32)
            tops.append(top)
            scaled.append(top * pgain_ref[...] * p_scale)
            at_row = jnp.dot(at_pos.astype(BF16), pattern4.astype(BF16), preferred_element_type=F32)
            at_rows.append(jnp.where(lane_t == row_t, at_row * qscale4, 0.0))
            lanes.append(((lane_t == row_t) & (lane_p == at)).astype(BF16))
        rows[...] = tops[0]
        top_copy = remote(rows, top_own, core_sem.at[0], core_sem.at[1], (s, f, 0))
        top_own[...] = tops[1]
        load_out.wait()
        both = jnp.concatenate(scaled, axis=0).astype(BF16)
        head_in = lax.dot_general(both, outp[...], NT, preferred_element_type=F32).astype(BF16)
        load_val.wait()
        gap = jnp.zeros((SEQ - (SL - HD), HD), BF16)

        def m_copy(k):
            return remote(msg.at[lax.rem(f + k, FEATS)], recv.at[f], p_send.at[k], p_recv.at[f], fdev(k))

        for k in range(FEATS):
            tail = val[k * SL + HD:(k + 1) * SL, :]
            weights = jnp.concatenate([val[k * SL:k * SL + HD, :]] + [tail, gap] * TGT, axis=0)
            got = lax.dot_general(head_in, weights, NT, preferred_element_type=F32)
            for group in range(2):
                part = got[8 * group:8 * group + 8]
                spread = jnp.where(lane_t == (row_t + 1) % TGT, part[:, HD:], 0.0)
                low = pltpu.roll(spread + at_rows[group], TGT, 0)
                msg[k, 8 * group:8 * group + 8] = jnp.where(row_t < TGT, part[:, :HD], low)

        def m_start(k, carry):
            m_copy(k).start()
            return carry

        lax.fori_loop(1, FEATS, m_start, 0)
        recv[f] = msg[f]
        top_copy.start()
        for k in range(FEATS):
            qslice[k] = qgain_ref[:, k * SL:(k + 1) * SL]
        gain = column(qslice[f])
        bases = []
        for group in range(2):
            for k in range(FEATS):
                gslice[k] = tops[group][:, k * SL:(k + 1) * SL]
            bases.append(lax.dot_general(gslice[f].astype(BF16), lanes[group], TN, preferred_element_type=F32))

        def m_wait_one(k, carry):
            j = lax.rem(f + k, FEATS)
            remote(msg.at[0], recv.at[j], p_send.at[0], p_recv.at[j], fdev(1)).wait_recv()
            return carry

        lax.fori_loop(1, FEATS, m_wait_one, 0)
        tail_t = lax.broadcasted_iota(jnp.int32, (SL - HD, COLS), 1) // SEQ
        for group in range(2):
            got = recv[:, 8 * group:8 * group + 8, :].reshape(FEATS * 8, COLS)
            got_row = lax.broadcasted_iota(jnp.int32, got.shape, 0) % 8
            got_t = lax.broadcasted_iota(jnp.int32, got.shape, 1) // SEQ
            low = jnp.where((got_row >= TGT) & (got_t == got_row - TGT), got, 0.0)
            high = pltpu.roll(low, FEATS * 8 - TGT, 0)
            left = got.astype(BF16)
            upper = lax.dot_general(left, high.astype(BF16), TN, preferred_element_type=F32)
            under = lax.dot_general(left, low.astype(BF16), TN, preferred_element_type=F32)
            tail = jnp.zeros((SL - HD, COLS), F32)
            for t in range(TGT):
                start = SEQ * ((t + 1) % TGT)
                tail = tail + jnp.where(tail_t == t, under[start:start + SL - HD, :], 0.0)
            new = bases[group] + jnp.concatenate([upper, tail], axis=0) * gain
            res[2 + group] = new.astype(BF16)
            if group == 0:
                for dy in (2, 1, 3, 0):
                    gin_copy(res.at[2], 2, dy, 0, 0).start()
            else:
                for dy in Y_FAR:
                    gin_copy(res.at[3], 3, dy, 0, 1).start()
                gin[0, gin_own, :] = res[3]
                out[own, :] = res[3]
        notes = [attribution_copy(res.at[2], out, 1, 3, 0, 0), attribution_copy(res.at[2], up, 0, 2, 0, 1),
                 attribution_copy(res.at[3], up, 0, 2, 1, 2)]
        for item in notes:
            item.start()

        def done():
            for dy in Y_FAR:
                e3_copy(dy).wait_send()
                gin_copy(res.at[3], 3, dy, 0, 1).wait_send()
            for dy in range(NY):
                gin_copy(res.at[2], 2, dy, 0, 0).wait_send()
            for dz in Z_FAR:
                e2_copy(dz).wait_send()
            top_copy.wait_send()
            for item in notes:
                item.wait_send()

            def m_done(k, carry):
                m_copy(k).wait_send()
                return carry

            lax.fori_loop(1, FEATS, m_done, 0)

        return done

    def release():
        pl.semaphore_signal(go_sem, inc=1, device_id=(s, f, 0), device_id_type=MESH)

    to_plane = 3 - s
    gin_slot = jnp.where(s >= 2, 0, 1)
    layer_now = jnp.where(s >= 2, 2, 1)
    group_now = jnp.where((s == 1) | (s == 2), 0, 1)

    def send_copies():
        items = [gin_copy(res.at[0], to_plane, dy, gin_slot, 2) for dy in (2, 1, 3, 0)]
        return items + [attribution_copy(res.at[0], out, 1, layer_now, group_now, 3)]

    def up_copy():
        return attribution_copy(res.at[0], up, 0, layer_now - 1, group_now, 4)

    def send_on(i):
        for item in send_copies():
            item.start()

        @pl.when(s > 0)
        def _():
            up_copy().start()

        @pl.when(s == 0)
        def _():
            up[own, :] = res[0]

    def send_done():
        for item in send_copies():
            item.wait_send()

        @pl.when(s > 0)
        def _():
            up_copy().wait_send()

    @pl.when(c == 0)
    def _():
        @pl.when(s == 3)
        def _():
            pick_rows()
            pl.semaphore_wait(barrier, 14)
            give = remote(rows, rows0, core_sem.at[0], core_sem.at[1], (s, f, 1))
            give.start()
            load_dec.wait()
            remote(rows, top_own, core_sem.at[0], core_sem.at[1], (s, f, 1)).wait_recv()
            top_scores(0)
            pl.semaphore_wait(go_sem, 1)
            give.wait_send()

        @pl.when(s < 3)
        def _():
            pl.semaphore_wait(barrier, 14)
            score_ref[...] = jnp.zeros_like(score_ref)
            load_dec.wait()
            sent = []
            pl.semaphore_wait(go_sem, 1)
            gather(up, 0, sent, add_up)
            pl.semaphore_wait(go_sem, 1)
            finish(sent)

        sent = []
        gather(out, 1, sent, add_out)
        grad_ref[...] = out[own, :].astype(F32)
        finish(sent)
        load_out.wait()
        load_val.wait()

    @pl.when(c == 1)
    def _():
        @pl.when(s == 3)
        def _():
            pick_rows()
            pl.semaphore_wait(barrier, 68)
            top_done = top_layer()
            load_dec.wait()
            step_done = layer_step(0)
            send_on(0)
            release()
            top_scores(1)
            sent = []
            gather(out, 1, sent, add_out, arrives=False)
            grad_ref[...] = out[own, :].astype(F32)
            top_done()
            step_done()
            finish(sent)

        @pl.when(s < 3)
        def _():
            pl.semaphore_wait(barrier, 47)
            weights_start()
            score_ref[...] = jnp.zeros_like(score_ref)
            load_dec.wait()
            step_done = layer_step(0)
            send_on(0)
            release()
            sent = []

            @pl.when(s > 0)
            def _():
                more = []
                gather(up, 0, more, add_up)
                finish(more)

            @pl.when(s == 0)
            def _():
                more = []
                gather(up, 0, more, add_up, arrives=False)
                finish(more)

            step_done()
            weights_done()

        @pl.when(s >= 2)
        def _():
            step_done = layer_step(1)
            last = attribution_copy(res.at[1], out, 1, 0, s - 2, 6)
            last.start()
            step_done()
            last.wait_send()

        @pl.when(s < 3)
        def _():
            release()
            sent = []
            gather(out, 1, sent, add_out)
            grad_ref[...] = out[own, :].astype(F32)
            finish(sent)

        send_done()


def pick_kernel(pos_hbm, count_hbm, ids_hbm, act_hbm, score_ref, grad_ref, out_ref, grad_out_ref,
                pos_ref, count_ref, ids_ref, act_ref, turned, picked, sem):
    pairs = ((pos_hbm, pos_ref), (count_hbm, count_ref), (ids_hbm, ids_ref), (act_hbm, act_ref))
    copies = [pltpu.make_async_copy(src, dst, sem.at[i]) for i, (src, dst) in enumerate(pairs)]
    for item in copies:
        item.start()
    turned[...] = score_ref[...].T
    grad_out_ref[0] = grad_ref[...].T.astype(BF16).reshape(TGT, SEQ, SL)
    for item in copies:
        item.wait()
    slots, width = ids_ref.shape[1], ids_ref.shape[2]
    for b in range(slots):
        at = pos_ref[0, b]
        for t in range(TGT):
            picked[t, b:b + 1, :] = turned[pl.ds(t * SEQ + at, 1), :]
    ids = ids_ref[0]
    live = lax.broadcasted_iota(jnp.int32, (slots, width), 0) < count_ref[0, 0]
    inner = ids % 128
    for t in range(TGT):
        low = jnp.take_along_axis(picked[t, :, :128], inner, axis=1, mode="promise_in_bounds")
        high = jnp.take_along_axis(picked[t, :, 128:], inner, axis=1, mode="promise_in_bounds")
        value = jnp.where(ids < 128, low, high) * act_ref[0]
        out_ref[0, t] = jnp.where(live, value, 0.0)


def body(
    target_ids, target_pos, target_gain, target_scale, encoder, post_gain, post_scale, out_proj, pattern,
    value_proj, pre_gain, pre_scale, decoder, block_ids, block_pos, block_act, block_count,
):
    vmem = pl.BlockSpec(memory_space=pltpu.VMEM)
    hbm = pl.BlockSpec(memory_space=pltpu.HBM)
    dma = pltpu.SemaphoreType.DMA
    shard = encoder.shape[0]
    features = decoder.shape[2]
    scores, grads = pl.pallas_call(
        main_kernel,
        out_shape=(
            jax.ShapeDtypeStruct((features, COLS), F32),
            jax.ShapeDtypeStruct((SL, COLS), F32),
        ),
        in_specs=[hbm] * 13,
        out_specs=(vmem, vmem),
        scratch_shapes=[
            pltpu.SMEM((2 * TGT,), jnp.int32),
            pltpu.SMEM((2 * TGT,), jnp.int32),
            pltpu.VMEM((1, D), F32),
            pltpu.VMEM((1, SEQ), F32),
            pltpu.VMEM((1, D), F32),
            pltpu.VMEM((1, SEQ), F32),
            pltpu.VMEM((1, D), F32),
            pltpu.VMEM((1, SEQ), F32),
            pltpu.VMEM((1, 1, SEQ, SEQ), BF16),
            pltpu.VMEM((shard, D), BF16),
            pltpu.VMEM((HD, D), BF16),
            pltpu.VMEM((D, HD), BF16),
            pltpu.VMEM((2, features, D), BF16),
            pltpu.VMEM((8, D), F32),
            pltpu.VMEM((8, D), F32),
            pltpu.VMEM((8, D), F32),
            pltpu.VMEM((NY, 8, QUARTER), F32),
            pltpu.VMEM((NZ, 8, QUARTER), F32),
            pltpu.VMEM((NY, 8, QUARTER), F32),
            pltpu.VMEM((8, QUARTER), F32),
            pltpu.VMEM((FEATS, 16, COLS), F32),
            pltpu.VMEM((FEATS, 16, COLS), F32),
            pltpu.VMEM((FEATS, 8, SL), F32),
            pltpu.VMEM((FEATS, 1, SL), F32),
            pltpu.VMEM((2, NZ, HD, WIN), BF16),
            pltpu.VMEM((2, BLOCK, NZ * HD), BF16),
            pltpu.VMEM((3, COLS, COLS), BF16),
            pltpu.VMEM((2, BLOCK + 2 * PAD, COLS), BF16),
            pltpu.VMEM((2, NZ, HD, COLS), BF16),
            pltpu.VMEM((2, NZ, HD, COLS), BF16),
            pltpu.VMEM((2, NZ * HD, COLS), BF16),
            pltpu.VMEM((2, NY, SL, COLS), BF16),
            pltpu.VMEM((2, NY, SL, COLS), BF16),
            pltpu.VMEM((4, SL, COLS), BF16),
            pltpu.VMEM((D, COLS), BF16),
            pltpu.VMEM((D, COLS), BF16),
            dma((4,)),
            dma((9,)),
            dma((2,)),
            dma((3, NZ)),
            dma((3, NZ)),
            dma((FEATS,)),
            dma((FEATS,)),
            dma((2, 3, NZ)),
            dma((2, 3, NZ)),
            dma((3, NY)),
            dma((2, NY)),
            dma((8,)),
            dma((2, NZ)),
            dma((2, NZ)),
            dma((2, NZ)),
            dma((2, NZ)),
            dma((2, NY)),
            dma((2, NY)),
            dma((2, FEATS)),
            dma((2, FEATS)),
            pltpu.SemaphoreType.REGULAR,
        ],
        compiler_params=pltpu.CompilerParams(
            collective_id=1, has_side_effects=True, vmem_limit_bytes=60 * 1024 * 1024
        ),
        name="chain",
    )(
        target_ids, target_pos, target_gain.reshape(1, D), target_scale.reshape(1, SEQ), post_gain, post_scale,
        pre_gain, pre_scale, pattern, encoder, out_proj, value_proj, decoder,
    )
    slots, width = block_ids.shape[1], block_ids.shape[2]
    return pl.pallas_call(
        pick_kernel,
        out_shape=(
            jax.ShapeDtypeStruct((1, TGT, slots, width), F32),
            jax.ShapeDtypeStruct((1, TGT, SEQ, SL), BF16),
        ),
        in_specs=[hbm] * 4 + [vmem] * 2,
        out_specs=(vmem, vmem),
        scratch_shapes=[
            pltpu.SMEM((1, slots), jnp.int32),
            pltpu.SMEM((1, 1), jnp.int32),
            pltpu.VMEM((1, slots, width), jnp.int32),
            pltpu.VMEM((1, slots, width), F32),
            pltpu.VMEM((COLS, features), F32),
            pltpu.VMEM((TGT, slots, features), F32),
            dma((4,)),
        ],
        name="pick",
    )(block_pos, block_count, block_ids, block_act, scores, grads)


def solution(mesh):
    in_specs = (
        P(),
        P(),
        P(),
        P(),
        P(("feat", "row"), None),
        P("section", None),
        P("section", None),
        P("section", "feat", None, None),
        P("section", "feat", None, None),
        P("section", "feat", None, None),
        P("section", None),
        P("section", None),
        P("section", None, "feat", None),
        P("section", "feat", None),
        P("section", "feat"),
        P("section", "feat", None),
        P("section", "feat"),
    )
    out_specs = (P("section", "row", "feat", None), P("section", "row", None, "feat"))
    return jax.shard_map(body, mesh=mesh, in_specs=in_specs, out_specs=out_specs, check_vma=False)
```

```python
import functools

import jax
import jax.numpy as jnp
from jax import lax
from jax.experimental import pallas as pl
from jax.experimental.pallas import tpu as pltpu
from jax.sharding import PartitionSpec as P

MESH = pl.DeviceIdType.MESH
F32 = jnp.float32
BF16 = jnp.bfloat16
NT = (((1,), (1,)), ((), ()))
TN = (((0,), (0,)), ((), ()))

D, HD, SEQ, FEATS, TGT = 4608, 128, 32, 32, 4
NZ, NY = 8, 4
SL = D // FEATS
COLS = TGT * SEQ
QUARTER = D // NY
BLOCK = D // NZ
WIN = 640
PAD = WIN - BLOCK
Z_ORDER = (1, 7, 2, 6, 3, 5, 4)
Z_FAR = (4, 3, 5, 2, 6, 1, 7)
Y_ORDER = (1, 3, 2)
Y_FAR = (2, 1, 3)


def main_kernel(
    ids_hbm, pos_hbm, tgain_hbm, tscale_hbm, pgain_hbm, pscale_hbm, qgain_hbm, qscale_hbm, pattern_hbm,
    enc_hbm, out_hbm, val_hbm, dec_hbm,
    score_ref, grad_ref,
    ids_ref, pos_ref, tgain_ref, tscale_ref, pgain_ref, pscale_ref, qgain_ref, qscale_ref, pattern_ref,
    enc, outp, val, dec, rows, rows0, top_own, e1, e2, e3, e2src, msg, recv, gslice, qslice,
    ow, vw, mixw, gin, hsrc, hpart, hm, gsrc, gpart, res, up, out,
    load_sem, small_sem, core_sem, e_send, e_recv, p_send, p_recv, w_send, w_recv, f_send, f_recv,
    gin_send, gin_recv, attr_send, h_send, h_recv, m_send, m_recv, y_send, y_recv, g_send, g_recv, go_sem,
):
    s = lax.axis_index("section")
    f = lax.axis_index("feat")
    c = lax.axis_index("row")
    z = f // NY
    y = f % NY

    def zdev(dz):
        return (s, lax.rem(z + dz, NZ) * NY + y, c)

    def ydev(dy):
        return (s, z * NY + lax.rem(y + dy, NY), c)

    def fdev(k):
        return (s, lax.rem(f + k, FEATS), c)

    def remote(src, dst, ss, rs, dev):
        return pltpu.make_async_remote_copy(
            src_ref=src, dst_ref=dst, send_sem=ss, recv_sem=rs, device_id=dev, device_id_type=MESH
        )

    load_enc = pltpu.make_async_copy(enc_hbm, enc, load_sem.at[0])
    load_out = pltpu.make_async_copy(out_hbm.at[0, 0], outp, load_sem.at[1])
    load_val = pltpu.make_async_copy(val_hbm.at[0, 0], val, load_sem.at[2])
    load_dec = pltpu.make_async_copy(dec_hbm.at[0], dec, load_sem.at[3])
    small = ((ids_hbm, ids_ref), (pos_hbm, pos_ref), (tgain_hbm, tgain_ref), (tscale_hbm, tscale_ref),
             (pgain_hbm, pgain_ref), (pscale_hbm, pscale_ref), (qgain_hbm, qgain_ref), (qscale_hbm, qscale_ref),
             (pattern_hbm, pattern_ref))
    small = [pltpu.make_async_copy(src, dst, small_sem.at[i]) for i, (src, dst) in enumerate(small)]

    @pl.when(s == 3)
    def _():
        load_enc.start()

    for item in small:
        item.start()
    load_out.start()
    load_val.start()
    load_dec.start()

    barrier = pltpu.get_barrier_semaphore()

    def hello(dev):
        pl.semaphore_signal(barrier, inc=1, device_id=dev, device_id_type=MESH)

    @pl.when(c == 0)
    def _():
        for dz in Z_ORDER:
            hello(zdev(dz))
        for dy in Y_ORDER:
            hello(ydev(dy))

    @pl.when(c == 1)
    def _():
        for dz in Z_ORDER:
            hello(zdev(dz))
        for dy in Y_ORDER:
            hello(ydev(dy))

        def other_planes(k, carry):
            q = lax.rem(s + k, 4)
            for dz in range(NZ):
                hello((q, lax.rem(z + dz, NZ) * NY + y, 1))
            for dy in Y_ORDER:
                hello((q, z * NY + lax.rem(y + dy, NY), 1))
            return carry

        lax.fori_loop(1, 4, other_planes, 0)

        @pl.when(s == 3)
        def _():
            def rest(dz, carry):
                for dy in Y_ORDER:
                    hello((s, lax.rem(z + dz, NZ) * NY + lax.rem(y + dy, NY), 1))
                return carry

            lax.fori_loop(1, NZ, rest, 0)

    for q in range(4):
        hello((q, f, 1 - c))
    for item in small:
        item.wait()

    lane_t = lax.broadcasted_iota(jnp.int32, (8, COLS), 1) // SEQ
    lane_p = lax.broadcasted_iota(jnp.int32, (8, COLS), 1) % SEQ
    row_t = lax.broadcasted_iota(jnp.int32, (8, COLS), 0)
    own_row = lax.broadcasted_iota(jnp.int32, (8, 1), 0)
    own = pl.ds(pl.multiple_of(f * SL, 16), SL)
    gin_own = pl.ds(pl.multiple_of(PAD + y * SL, 16), SL)
    pattern = pattern_ref[0, 0].astype(F32)

    def column(row):
        n = row.shape[1]
        eye = lax.broadcasted_iota(jnp.int32, (n, n), 0) == lax.broadcasted_iota(jnp.int32, (n, n), 1)
        return jnp.sum(jnp.where(eye, jnp.broadcast_to(row, (n, n)), 0.0), axis=1, keepdims=True)

    def pick_rows():
        load_enc.wait()
        base = (f * 2 + c) * enc.shape[0]
        wanted = jnp.full((8, 1), -1, jnp.int32)
        for t in range(8):
            wanted = jnp.where(own_row == t, ids_ref[t] - base, wanted)
        hit = lax.broadcasted_iota(jnp.int32, (8, enc.shape[0]), 1) == wanted
        rows[...] = jnp.dot(hit.astype(BF16), enc[...], preferred_element_type=F32)

    def positions(group):
        at = jnp.full((8, 1), -1, jnp.int32)
        for t in range(TGT):
            at = jnp.where(own_row == t, pos_ref[t + TGT * group], at)
        return at

    def top_scores(group):
        at_lane = ((lane_t == row_t) & (lane_p == positions(group))).astype(F32)
        part = lax.dot_general(dec[1], top_own[...].astype(BF16), NT, preferred_element_type=F32)
        score_ref[...] = jnp.dot(part, at_lane, preferred_element_type=F32, precision=lax.Precision.HIGHEST)

    def gather(full, k, sent, use, arrives=True):
        def copy(b, dev, i):
            part = full.at[pl.ds(pl.multiple_of(b * SL, 16), SL)]
            return remote(part, part, g_send.at[k, i], g_recv.at[k, b], dev)

        def start(item):
            item.start()
            sent.append(item)

        def forward(b, i):
            for j, dy in enumerate(Y_ORDER):
                start(copy(b, ydev(dy), 3 * i + j))

        if arrives:
            copy(f, ydev(1), 0).wait_recv()
        forward(f, 0)
        for i, dz in enumerate(Z_ORDER):
            start(copy(f, zdev(dz), 24 + i))
        for i, dz in enumerate(Z_ORDER):
            b = lax.rem(z + NZ - dz, NZ) * NY + y
            copy(b, ydev(1), 0).wait_recv()
            forward(b, 1 + i)
        span = 2 * NY * SL
        for dq in (0, 1, 3, 2):
            q = lax.rem(z // 2 + dq, NZ // 2)
            for half in range(2):
                for dy in Y_ORDER:
                    b = (2 * q + half) * NY + lax.rem(y + dy, NY)
                    copy(b, ydev(1), 0).wait_recv()
            part = pl.ds(pl.multiple_of(q * span, 128), span)
            use(part, full[part, :])

    def add_up(part, block):
        score_ref[...] += jnp.dot(dec[1, :, part], block, preferred_element_type=F32)

    def add_out(part, block):
        score_ref[...] += jnp.dot(dec[0, :, part], block, preferred_element_type=F32)

    def finish(sent):
        for item in sent:
            item.wait_send()

    def attribution_copy(src, full, k, layer, group, i):
        return remote(src, full.at[own], attr_send.at[i], g_recv.at[k, f], (layer, f, group))

    def gin_copy(src, plane, dy, i, j):
        dev = (plane, z * NY + lax.rem(y + dy, NY), 1)
        return remote(src, gin.at[i, gin_own], gin_send.at[j, dy], gin_recv.at[i, y], dev)

    def gin_wait(i, dy):
        j = lax.rem(y + dy, NY)
        part = gin.at[i, pl.ds(pl.multiple_of(PAD + j * SL, 16), SL)]
        remote(part, part, gin_send.at[0, 0], gin_recv.at[i, j], ydev(1)).wait_recv()

    home_slot = jnp.where(s == 0, 1, 0)

    def w_copy(dz, kind):
        zz = lax.rem(z + dz, NZ)
        ss, rs = w_send.at[kind, dz], w_recv.at[kind, z]
        if kind == 0:
            first = pl.multiple_of(zz * BLOCK - PAD * (zz % 2), 128)
            return remote(outp.at[:, pl.ds(first, WIN)], ow.at[home_slot, z], ss, rs, zdev(dz))
        src = val.at[pl.ds(pl.multiple_of(zz * BLOCK, 16), BLOCK)]
        dst = vw.at[home_slot, :, pl.ds(pl.multiple_of(z * HD, 128), HD)]
        return remote(src, dst, ss, rs, zdev(dz))

    def on_copy(kind, di):
        ref = (ow, vw, mixw)[kind].at[home_slot]
        dest = 2 if di == 1 else jnp.where(s == 1, 0, 3)
        return remote(ref, ref, f_send.at[di, kind], f_recv.at[home_slot, kind], (dest, f, 1))

    def on_start(kind):
        on_copy(kind, 0).start()

        @pl.when(s == 0)
        def _():
            on_copy(kind, 1).start()

    def w_arrived(kind):
        for dz in Z_ORDER:
            zz = lax.rem(z + dz, NZ)
            if kind == 0:
                part = ow.at[home_slot, zz]
            else:
                part = vw.at[home_slot, :, pl.ds(pl.multiple_of(zz * HD, 128), HD)]
            remote(part, part, w_send.at[kind, 0], w_recv.at[kind, zz], ydev(1)).wait_recv()

    def weights_start():
        load_out.wait()
        outp[...] = (outp[...].astype(F32) * pgain_ref[...]).astype(BF16)
        for dz in Z_FAR:
            w_copy(dz, 0).start()
        ow[home_slot, z] = outp[:, pl.ds(pl.multiple_of(z * BLOCK - PAD * (z % 2), 128), WIN)]
        scaled = pattern * column(pscale_ref[...]) * qscale_ref[...]
        wide = jnp.concatenate([scaled] * TGT, axis=1)
        wide = jnp.concatenate([wide] * TGT, axis=0)
        same = (lax.broadcasted_iota(jnp.int32, wide.shape, 0) // SEQ
                == lax.broadcasted_iota(jnp.int32, wide.shape, 1) // SEQ)
        mixw[home_slot] = jnp.where(same, wide, 0.0).astype(BF16)
        on_start(2)
        load_val.wait()
        for k in range(FEATS):
            part = slice(k * SL, (k + 1) * SL)
            val[part, :] = (val[part, :].astype(F32) * column(qgain_ref[:, part])).astype(BF16)
        for dz in Z_FAR:
            w_copy(dz, 1).start()
        vw[home_slot, :, pl.ds(pl.multiple_of(z * HD, 128), HD)] = val[pl.ds(pl.multiple_of(z * BLOCK, 16), BLOCK), :]
        w_arrived(0)
        on_start(0)
        w_arrived(1)
        on_start(1)

    def weights_done():
        for kind in range(2):
            for dz in Z_FAR:
                w_copy(dz, kind).wait_send()
        for kind in range(3):
            on_copy(kind, 0).wait_send()

            @pl.when(s == 0)
            def _():
                on_copy(kind, 1).wait_send()

    def w_wait(i, kind):
        def one():
            ref = (ow, vw, mixw)[kind].at[i]
            remote(ref, ref, f_send.at[0, kind], f_recv.at[i, kind], ydev(1)).wait_recv()

        if i == 1:
            one()
        else:
            pl.when((s == 0) | (s == 3))(one)

    def layer_step(i):
        gin[i, 0:PAD] = jnp.zeros((PAD, COLS), BF16)
        gin[i, PAD + BLOCK:] = jnp.zeros((PAD, COLS), BF16)
        w_wait(i, 0)
        w_wait(i, 2)
        for dy in Y_ORDER:
            gin_wait(i, dy)
        if i == 1:
            gin_wait(i, 0)
        else:
            @pl.when(s < 3)
            def _():
                gin_wait(i, 0)

        block = gin[i, pl.ds(pl.multiple_of(PAD * (1 - z % 2), 16), WIN), :]

        def h_copy(dz):
            zz = lax.rem(z + dz, NZ)
            return remote(hsrc.at[i, zz], hpart.at[i, z], h_send.at[i, dz], h_recv.at[i, z], zdev(dz))

        for dz in Z_FAR:
            zz = lax.rem(z + dz, NZ)
            hsrc[i, zz] = jnp.dot(ow[i, zz], block, preferred_element_type=F32).astype(BF16)
            h_copy(dz).start()
        total = jnp.dot(ow[i, z], block, preferred_element_type=F32)
        for dz in Z_ORDER:
            zz = lax.rem(z + dz, NZ)
            remote(hpart.at[i, zz], hpart.at[i, zz], h_send.at[i, 0], h_recv.at[i, zz], ydev(1)).wait_recv()
            total = total + hpart[i, zz].astype(F32)
        mixed = jnp.dot(total.astype(BF16), mixw[i], preferred_element_type=F32).astype(BF16)
        mine = pl.ds(pl.multiple_of(z * HD, 128), HD)
        hm[i, mine, :] = mixed

        def hm_copy(dz):
            return remote(hm.at[i, mine], hm.at[i, mine], m_send.at[i, dz], m_recv.at[i, z], zdev(dz))

        for dz in Z_FAR:
            hm_copy(dz).start()
        w_wait(i, 1)
        for dz in Z_ORDER:
            zz = lax.rem(z + dz, NZ)
            part = hm.at[i, pl.ds(pl.multiple_of(zz * HD, 128), HD)]
            remote(part, part, m_send.at[i, 0], m_recv.at[i, zz], ydev(1)).wait_recv()

        def g_part(dy):
            yy = lax.rem(y + dy, NY)
            weights = vw[i, pl.ds(pl.multiple_of(yy * SL, 16), SL), :]
            return jnp.dot(weights, hm[i], preferred_element_type=F32)

        def gp_copy(dy):
            yy = lax.rem(y + dy, NY)
            return remote(gsrc.at[i, yy], gpart.at[i, y], y_send.at[i, dy], y_recv.at[i, y], ydev(dy))

        for dy in Y_FAR:
            gsrc[i, lax.rem(y + dy, NY)] = g_part(dy).astype(BF16)
            gp_copy(dy).start()
        total = g_part(0) + gin[i, gin_own, :].astype(F32)
        for dy in Y_ORDER:
            yy = lax.rem(y + dy, NY)
            remote(gpart.at[i, yy], gpart.at[i, yy], y_send.at[i, 0], y_recv.at[i, yy], ydev(1)).wait_recv()
            total = total + gpart[i, yy].astype(F32)
        res[i] = total.astype(BF16)

        def done():
            for dz in Z_FAR:
                h_copy(dz).wait_send()
                hm_copy(dz).wait_send()
            for dy in Y_FAR:
                gp_copy(dy).wait_send()

        return done

    def top_layer():
        me = y

        def quarter(j):
            return rows.at[:, pl.ds(pl.multiple_of(j * QUARTER, 128), QUARTER)]

        def e_copy(stage, src, dst, k, slot, dev):
            return remote(src, dst.at[slot], e_send.at[stage, k], e_recv.at[stage, slot], dev)

        remote(rows0, rows0, core_sem.at[0], core_sem.at[1], (s, f, 0)).wait_recv()
        rows[...] = rows[...] + rows0[...]

        def e1_copy(dy):
            return e_copy(0, quarter(lax.rem(y + dy, NY)), e1, dy, me, ydev(dy))

        for dy in Y_FAR:
            e1_copy(dy).start()
        total = quarter(me)[...]
        for dy in Y_ORDER:
            j = lax.rem(y + dy, NY)
            e_copy(0, e2src, e1, 0, j, ydev(1)).wait_recv()
            total = total + e1[j]
        e2src[...] = total

        def e2_copy(dz):
            return e_copy(1, e2src, e2, dz, z, zdev(dz))

        for dz in Z_FAR:
            e2_copy(dz).start()
        for dz in Z_ORDER:
            j = lax.rem(z + dz, NZ)
            e_copy(1, e2src, e2, 0, j, ydev(1)).wait_recv()
            total = total + e2[j]
        e3[me] = total

        def e3_copy(dy):
            return e_copy(2, e3.at[me], e3, dy, me, ydev(dy))

        for dy in Y_FAR:
            e3_copy(dy).start()
        for dy in Y_ORDER:
            e_copy(2, e2src, e3, 0, lax.rem(y + dy, NY), ydev(1)).wait_recv()
        for dy in Y_FAR:
            e1_copy(dy).wait_send()
        raw = jnp.concatenate([e3[k] for k in range(NY)], axis=1)

        tops, scaled, at_rows, lanes = [], [], [], []
        pattern4 = jnp.concatenate([pattern] * TGT, axis=1)
        qscale4 = jnp.concatenate([qscale_ref[...]] * TGT, axis=1)
        for group in range(2):
            part = raw if group == 0 else pltpu.roll(raw, TGT, 0)
            part = jnp.where(own_row < TGT, part, 0.0)
            at = positions(group)
            at_pos = lax.broadcasted_iota(jnp.int32, (8, SEQ), 1) == at
            t_scale = jnp.sum(jnp.where(at_pos, jnp.broadcast_to(tscale_ref[...], (8, SEQ)), 0.0),
                              axis=1, keepdims=True)
            p_scale = jnp.sum(jnp.where(at_pos, jnp.broadcast_to(pscale_ref[...], (8, SEQ)), 0.0),
                              axis=1, keepdims=True)
            top = (part * tgain_ref[...] * t_scale).astype(BF16).astype(F32)
            tops.append(top)
            scaled.append(top * pgain_ref[...] * p_scale)
            at_row = jnp.dot(at_pos.astype(BF16), pattern4.astype(BF16), preferred_element_type=F32)
            at_rows.append(jnp.where(lane_t == row_t, at_row * qscale4, 0.0))
            lanes.append(((lane_t == row_t) & (lane_p == at)).astype(BF16))
        rows[...] = tops[0]
        top_copy = remote(rows, top_own, core_sem.at[0], core_sem.at[1], (s, f, 0))
        top_own[...] = tops[1]
        load_out.wait()
        both = jnp.concatenate(scaled, axis=0).astype(BF16)
        head_in = lax.dot_general(both, outp[...], NT, preferred_element_type=F32).astype(BF16)
        load_val.wait()
        gap = jnp.zeros((SEQ - (SL - HD), HD), BF16)

        def m_copy(k):
            return remote(msg.at[lax.rem(f + k, FEATS)], recv.at[f], p_send.at[k], p_recv.at[f], fdev(k))

        for k in range(FEATS):
            tail = val[k * SL + HD:(k + 1) * SL, :]
            weights = jnp.concatenate([val[k * SL:k * SL + HD, :]] + [tail, gap] * TGT, axis=0)
            got = lax.dot_general(head_in, weights, NT, preferred_element_type=F32)
            for group in range(2):
                part = got[8 * group:8 * group + 8]
                spread = jnp.where(lane_t == (row_t + 1) % TGT, part[:, HD:], 0.0)
                low = pltpu.roll(spread + at_rows[group], TGT, 0)
                msg[k, 8 * group:8 * group + 8] = jnp.where(row_t < TGT, part[:, :HD], low)

        def m_start(k, carry):
            m_copy(k).start()
            return carry

        lax.fori_loop(1, FEATS, m_start, 0)
        recv[f] = msg[f]
        top_copy.start()
        for k in range(FEATS):
            qslice[k] = qgain_ref[:, k * SL:(k + 1) * SL]
        gain = column(qslice[f])
        bases = []
        for group in range(2):
            for k in range(FEATS):
                gslice[k] = tops[group][:, k * SL:(k + 1) * SL]
            bases.append(lax.dot_general(gslice[f].astype(BF16), lanes[group], TN, preferred_element_type=F32))

        def m_wait_one(k, carry):
            j = lax.rem(f + k, FEATS)
            remote(msg.at[0], recv.at[j], p_send.at[0], p_recv.at[j], fdev(1)).wait_recv()
            return carry

        lax.fori_loop(1, FEATS, m_wait_one, 0)
        tail_t = lax.broadcasted_iota(jnp.int32, (SL - HD, COLS), 1) // SEQ
        for group in range(2):
            got = recv[:, 8 * group:8 * group + 8, :].reshape(FEATS * 8, COLS)
            got_row = lax.broadcasted_iota(jnp.int32, got.shape, 0) % 8
            got_t = lax.broadcasted_iota(jnp.int32, got.shape, 1) // SEQ
            low = jnp.where((got_row >= TGT) & (got_t == got_row - TGT), got, 0.0)
            high = pltpu.roll(low, FEATS * 8 - TGT, 0)
            left = got.astype(BF16)
            upper = lax.dot_general(left, high.astype(BF16), TN, preferred_element_type=F32)
            under = lax.dot_general(left, low.astype(BF16), TN, preferred_element_type=F32)
            tail = jnp.zeros((SL - HD, COLS), F32)
            for t in range(TGT):
                start = SEQ * ((t + 1) % TGT)
                tail = tail + jnp.where(tail_t == t, under[start:start + SL - HD, :], 0.0)
            new = bases[group] + jnp.concatenate([upper, tail], axis=0) * gain
            res[2 + group] = new.astype(BF16)
            if group == 0:
                for dy in (2, 1, 3, 0):
                    gin_copy(res.at[2], 2, dy, 0, 0).start()
            else:
                for dy in Y_FAR:
                    gin_copy(res.at[3], 3, dy, 0, 1).start()
                gin[0, gin_own, :] = res[3]
                out[own, :] = res[3]
        notes = [attribution_copy(res.at[2], out, 1, 3, 0, 0), attribution_copy(res.at[2], up, 0, 2, 0, 1),
                 attribution_copy(res.at[3], up, 0, 2, 1, 2)]
        for item in notes:
            item.start()

        def done():
            for dy in Y_FAR:
                e3_copy(dy).wait_send()
                gin_copy(res.at[3], 3, dy, 0, 1).wait_send()
            for dy in range(NY):
                gin_copy(res.at[2], 2, dy, 0, 0).wait_send()
            for dz in Z_FAR:
                e2_copy(dz).wait_send()
            top_copy.wait_send()
            for item in notes:
                item.wait_send()

            def m_done(k, carry):
                m_copy(k).wait_send()
                return carry

            lax.fori_loop(1, FEATS, m_done, 0)

        return done

    def release():
        pl.semaphore_signal(go_sem, inc=1, device_id=(s, f, 0), device_id_type=MESH)

    to_plane = 3 - s
    gin_slot = jnp.where(s >= 2, 0, 1)
    layer_now = jnp.where(s >= 2, 2, 1)
    group_now = jnp.where((s == 1) | (s == 2), 0, 1)

    def send_copies():
        items = [gin_copy(res.at[0], to_plane, dy, gin_slot, 2) for dy in (2, 1, 3, 0)]
        return items + [attribution_copy(res.at[0], out, 1, layer_now, group_now, 3)]

    def up_copy():
        return attribution_copy(res.at[0], up, 0, layer_now - 1, group_now, 4)

    def send_on(i):
        for item in send_copies():
            item.start()

        @pl.when(s > 0)
        def _():
            up_copy().start()

        @pl.when(s == 0)
        def _():
            up[own, :] = res[0]

    def send_done():
        for item in send_copies():
            item.wait_send()

        @pl.when(s > 0)
        def _():
            up_copy().wait_send()

    @pl.when(c == 0)
    def _():
        @pl.when(s == 3)
        def _():
            pick_rows()
            pl.semaphore_wait(barrier, 14)
            give = remote(rows, rows0, core_sem.at[0], core_sem.at[1], (s, f, 1))
            give.start()
            load_dec.wait()
            remote(rows, top_own, core_sem.at[0], core_sem.at[1], (s, f, 1)).wait_recv()
            top_scores(0)
            pl.semaphore_wait(go_sem, 1)
            give.wait_send()

        @pl.when(s < 3)
        def _():
            pl.semaphore_wait(barrier, 14)
            score_ref[...] = jnp.zeros_like(score_ref)
            load_dec.wait()
            sent = []
            pl.semaphore_wait(go_sem, 1)
            gather(up, 0, sent, add_up)
            pl.semaphore_wait(go_sem, 1)
            finish(sent)

        sent = []
        gather(out, 1, sent, add_out)
        grad_ref[...] = out[own, :].astype(F32)
        finish(sent)
        load_out.wait()
        load_val.wait()

    @pl.when(c == 1)
    def _():
        @pl.when(s == 3)
        def _():
            pick_rows()
            pl.semaphore_wait(barrier, 68)
            top_done = top_layer()
            load_dec.wait()
            step_done = layer_step(0)
            send_on(0)
            release()
            top_scores(1)
            sent = []
            gather(out, 1, sent, add_out, arrives=False)
            grad_ref[...] = out[own, :].astype(F32)
            top_done()
            step_done()
            finish(sent)

        @pl.when(s < 3)
        def _():
            pl.semaphore_wait(barrier, 47)
            weights_start()
            score_ref[...] = jnp.zeros_like(score_ref)
            load_dec.wait()
            step_done = layer_step(0)
            send_on(0)
            release()
            release()
            sent = []

            @pl.when(s > 0)
            def _():
                more = []
                gather(up, 0, more, add_up)
                finish(more)

            @pl.when(s == 0)
            def _():
                more = []
                gather(up, 0, more, add_up, arrives=False)
                finish(more)

            step_done()
            weights_done()

        @pl.when(s >= 2)
        def _():
            step_done = layer_step(1)
            last = attribution_copy(res.at[1], out, 1, 0, s - 2, 6)
            last.start()
            step_done()
            last.wait_send()

        @pl.when(s < 3)
        def _():
            sent = []
            gather(out, 1, sent, add_out)
            grad_ref[...] = out[own, :].astype(F32)
            finish(sent)

        send_done()


def pick_kernel(pos_hbm, count_hbm, ids_hbm, act_hbm, score_ref, grad_ref, out_ref, grad_out_ref,
                pos_ref, count_ref, ids_ref, act_ref, turned, picked, sem):
    pairs = ((pos_hbm, pos_ref), (count_hbm, count_ref), (ids_hbm, ids_ref), (act_hbm, act_ref))
    copies = [pltpu.make_async_copy(src, dst, sem.at[i]) for i, (src, dst) in enumerate(pairs)]
    for item in copies:
        item.start()
    turned[...] = score_ref[...].T
    grad_out_ref[0] = grad_ref[...].T.astype(BF16).reshape(TGT, SEQ, SL)
    for item in copies:
        item.wait()
    slots, width = ids_ref.shape[1], ids_ref.shape[2]
    for b in range(slots):
        at = pos_ref[0, b]
        for t in range(TGT):
            picked[t, b:b + 1, :] = turned[pl.ds(t * SEQ + at, 1), :]
    ids = ids_ref[0]
    live = lax.broadcasted_iota(jnp.int32, (slots, width), 0) < count_ref[0, 0]
    inner = ids % 128
    for t in range(TGT):
        low = jnp.take_along_axis(picked[t, :, :128], inner, axis=1, mode="promise_in_bounds")
        high = jnp.take_along_axis(picked[t, :, 128:], inner, axis=1, mode="promise_in_bounds")
        value = jnp.where(ids < 128, low, high) * act_ref[0]
        out_ref[0, t] = jnp.where(live, value, 0.0)


def body(
    target_ids, target_pos, target_gain, target_scale, encoder, post_gain, post_scale, out_proj, pattern,
    value_proj, pre_gain, pre_scale, decoder, block_ids, block_pos, block_act, block_count,
):
    vmem = pl.BlockSpec(memory_space=pltpu.VMEM)
    hbm = pl.BlockSpec(memory_space=pltpu.HBM)
    dma = pltpu.SemaphoreType.DMA
    shard = encoder.shape[0]
    features = decoder.shape[2]
    scores, grads = pl.pallas_call(
        main_kernel,
        out_shape=(
            jax.ShapeDtypeStruct((features, COLS), F32),
            jax.ShapeDtypeStruct((SL, COLS), F32),
        ),
        in_specs=[hbm] * 13,
        out_specs=(vmem, vmem),
        scratch_shapes=[
            pltpu.SMEM((2 * TGT,), jnp.int32),
            pltpu.SMEM((2 * TGT,), jnp.int32),
            pltpu.VMEM((1, D), F32),
            pltpu.VMEM((1, SEQ), F32),
            pltpu.VMEM((1, D), F32),
            pltpu.VMEM((1, SEQ), F32),
            pltpu.VMEM((1, D), F32),
            pltpu.VMEM((1, SEQ), F32),
            pltpu.VMEM((1, 1, SEQ, SEQ), BF16),
            pltpu.VMEM((shard, D), BF16),
            pltpu.VMEM((HD, D), BF16),
            pltpu.VMEM((D, HD), BF16),
            pltpu.VMEM((2, features, D), BF16),
            pltpu.VMEM((8, D), F32),
            pltpu.VMEM((8, D), F32),
            pltpu.VMEM((8, D), F32),
            pltpu.VMEM((NY, 8, QUARTER), F32),
            pltpu.VMEM((NZ, 8, QUARTER), F32),
            pltpu.VMEM((NY, 8, QUARTER), F32),
            pltpu.VMEM((8, QUARTER), F32),
            pltpu.VMEM((FEATS, 16, COLS), F32),
            pltpu.VMEM((FEATS, 16, COLS), F32),
            pltpu.VMEM((FEATS, 8, SL), F32),
            pltpu.VMEM((FEATS, 1, SL), F32),
            pltpu.VMEM((2, NZ, HD, WIN), BF16),
            pltpu.VMEM((2, BLOCK, NZ * HD), BF16),
            pltpu.VMEM((2, COLS, COLS), BF16),
            pltpu.VMEM((2, BLOCK + 2 * PAD, COLS), BF16),
            pltpu.VMEM((2, NZ, HD, COLS), BF16),
            pltpu.VMEM((2, NZ, HD, COLS), BF16),
            pltpu.VMEM((2, NZ * HD, COLS), BF16),
            pltpu.VMEM((2, NY, SL, COLS), BF16),
            pltpu.VMEM((2, NY, SL, COLS), BF16),
            pltpu.VMEM((4, SL, COLS), BF16),
            pltpu.VMEM((D, COLS), BF16),
            pltpu.VMEM((D, COLS), BF16),
            dma((4,)),
            dma((9,)),
            dma((2,)),
            dma((3, NZ)),
            dma((3, NZ)),
            dma((FEATS,)),
            dma((FEATS,)),
            dma((2, NZ)),
            dma((2, NZ)),
            dma((2, 3)),
            dma((2, 3)),
            dma((3, NY)),
            dma((2, NY)),
            dma((8,)),
            dma((2, NZ)),
            dma((2, NZ)),
            dma((2, NZ)),
            dma((2, NZ)),
            dma((2, NY)),
            dma((2, NY)),
            dma((2, FEATS)),
            dma((2, FEATS)),
            pltpu.SemaphoreType.REGULAR,
        ],
        compiler_params=pltpu.CompilerParams(
            collective_id=1, has_side_effects=True, vmem_limit_bytes=60 * 1024 * 1024
        ),
        name="chain",
    )(
        target_ids, target_pos, target_gain.reshape(1, D), target_scale.reshape(1, SEQ), post_gain, post_scale,
        pre_gain, pre_scale, pattern, encoder, out_proj, value_proj, decoder,
    )
    slots, width = block_ids.shape[1], block_ids.shape[2]
    return pl.pallas_call(
        pick_kernel,
        out_shape=(
            jax.ShapeDtypeStruct((1, TGT, slots, width), F32),
            jax.ShapeDtypeStruct((1, TGT, SEQ, SL), BF16),
        ),
        in_specs=[hbm] * 4 + [vmem] * 2,
        out_specs=(vmem, vmem),
        scratch_shapes=[
            pltpu.SMEM((1, slots), jnp.int32),
            pltpu.SMEM((1, 1), jnp.int32),
            pltpu.VMEM((1, slots, width), jnp.int32),
            pltpu.VMEM((1, slots, width), F32),
            pltpu.VMEM((COLS, features), F32),
            pltpu.VMEM((TGT, slots, features), F32),
            dma((4,)),
        ],
        name="pick",
    )(block_pos, block_count, block_ids, block_act, scores, grads)


def solution(mesh):
    in_specs = (
        P(),
        P(),
        P(),
        P(),
        P(("feat", "row"), None),
        P("section", None),
        P("section", None),
        P("section", "feat", None, None),
        P("section", "feat", None, None),
        P("section", "feat", None, None),
        P("section", None),
        P("section", None),
        P("section", None, "feat", None),
        P("section", "feat", None),
        P("section", "feat"),
        P("section", "feat", None),
        P("section", "feat"),
    )
    out_specs = (P("section", "row", "feat", None), P("section", "row", None, "feat"))
    return jax.shard_map(body, mesh=mesh, in_specs=in_specs, out_specs=out_specs, check_vma=False)
```

```python
import functools

import jax
import jax.numpy as jnp
from jax import lax
from jax.experimental import pallas as pl
from jax.experimental.pallas import tpu as pltpu
from jax.sharding import PartitionSpec as P

MESH = pl.DeviceIdType.MESH
F32 = jnp.float32
BF16 = jnp.bfloat16
NT = (((1,), (1,)), ((), ()))
TN = (((0,), (0,)), ((), ()))

D, HD, SEQ, FEATS, TGT = 4608, 128, 32, 32, 4
NZ, NY = 8, 4
SL = D // FEATS
COLS = TGT * SEQ
QUARTER = D // NY
BLOCK = D // NZ
WIN = 640
PAD = WIN - BLOCK
SPLIT = 96
Z_ORDER = (1, 7, 2, 6, 3, 5, 4)
Z_FAR = (4, 3, 5, 2, 6, 1, 7)
Y_ORDER = (1, 3, 2)
Y_FAR = (2, 1, 3)


def main_kernel(
    ids_hbm, pos_hbm, tgain_hbm, tscale_hbm, pgain_hbm, pscale_hbm, qgain_hbm, qscale_hbm, pattern_hbm,
    enc_hbm, out_hbm, val_hbm, dec_hbm,
    score_ref, grad_ref,
    ids_ref, pos_ref, tgain_ref, tscale_ref, pgain_ref, pscale_ref, qgain_ref, qscale_ref, pattern_ref,
    enc, outp, val, dec, rows, rows0, top_own, epack, e1, e2, e3, e2src, msg, recv, gslice, qslice,
    ow, vw, mixw, gin, hsrc, hpart, hm, gsrc, gpart, res, up, out,
    load_sem, small_sem, core_sem, e_send, e_recv, p_send, p_recv, w_send, w_recv, f_send, f_recv, o_send, o_recv,
    gin_send, gin_recv, attr_send, h_send, h_recv, m_send, m_recv, y_send, y_recv, g_send, g_recv, l_send, l_recv, go_sem,
):
    s = lax.axis_index("section")
    f = lax.axis_index("feat")
    c = lax.axis_index("row")
    z = f // NY
    y = f % NY

    def zdev(dz):
        return (s, lax.rem(z + dz, NZ) * NY + y, c)

    def ydev(dy):
        return (s, z * NY + lax.rem(y + dy, NY), c)

    def fdev(k):
        return (s, lax.rem(f + k, FEATS), c)

    def remote(src, dst, ss, rs, dev):
        return pltpu.make_async_remote_copy(
            src_ref=src, dst_ref=dst, send_sem=ss, recv_sem=rs, device_id=dev, device_id_type=MESH
        )

    enc_part = enc.shape[0] // 4
    load_enc = [
        pltpu.make_async_copy(enc_hbm.at[pl.ds(k * enc_part, enc_part)], enc.at[pl.ds(k * enc_part, enc_part)],
                              load_sem.at[4 + k])
        for k in range(4)
    ]
    load_out = pltpu.make_async_copy(out_hbm.at[0, 0], outp, load_sem.at[1])
    load_val = pltpu.make_async_copy(val_hbm.at[0, 0], val, load_sem.at[2])
    load_dec = pltpu.make_async_copy(dec_hbm.at[0], dec, load_sem.at[3])
    small = ((ids_hbm, ids_ref), (pos_hbm, pos_ref), (tgain_hbm, tgain_ref), (tscale_hbm, tscale_ref),
             (pgain_hbm, pgain_ref), (pscale_hbm, pscale_ref), (qgain_hbm, qgain_ref), (qscale_hbm, qscale_ref),
             (pattern_hbm, pattern_ref))
    small = [pltpu.make_async_copy(src, dst, small_sem.at[i]) for i, (src, dst) in enumerate(small)]

    @pl.when(s == 3)
    def _():
        for item in load_enc:
            item.start()

    barrier = pltpu.get_barrier_semaphore()

    def hello(dev):
        pl.semaphore_signal(barrier, inc=1, device_id=dev, device_id_type=MESH)

    for dz in Z_FAR:
        hello(zdev(dz))
    for dy in Y_FAR:
        hello(ydev(dy))

    def column_peers(plane, core):
        for dz in Z_FAR:
            hello((plane, lax.rem(z + dz, NZ) * NY + y, core))

    def row_peers(plane, core):
        for dy in Y_FAR:
            hello((plane, z * NY + lax.rem(y + dy, NY), core))

    @pl.when((c == 0) & (s == 0))
    def _():
        column_peers(2, 1)
        row_peers(2, 1)

    @pl.when(c == 1)
    def _():
        @pl.when(s == 2)
        def _():
            column_peers(0, 0)
            row_peers(0, 0)

        for k in (2, 1, 3):
            q = lax.rem(s + k, 4)
            row_peers(q, 1)
            hello((q, f, 1))

    for q in range(4):
        hello((q, f, 1 - c))

    for item in small:
        item.start()

    @pl.when((s < 3) & (c == 1))
    def _():
        load_out.start()
        load_val.start()

    @pl.when((s < 3) & (c == 0))
    def _():
        load_dec.start()

    for item in small:
        item.wait()

    lane_t = lax.broadcasted_iota(jnp.int32, (8, COLS), 1) // SEQ
    lane_p = lax.broadcasted_iota(jnp.int32, (8, COLS), 1) % SEQ
    row_t = lax.broadcasted_iota(jnp.int32, (8, COLS), 0)
    own_row = lax.broadcasted_iota(jnp.int32, (8, 1), 0)
    own = pl.ds(pl.multiple_of(f * SL, 16), SL)
    gin_own = pl.ds(pl.multiple_of(PAD + y * SL, 16), SL)
    pattern = pattern_ref[0, 0].astype(F32)

    def column(row):
        n = row.shape[1]
        eye = lax.broadcasted_iota(jnp.int32, (n, n), 0) == lax.broadcasted_iota(jnp.int32, (n, n), 1)
        return jnp.sum(jnp.where(eye, jnp.broadcast_to(row, (n, n)), 0.0), axis=1, keepdims=True)

    def pick_rows():
        for item in load_enc:
            item.wait()

        @pl.when(c == 1)
        def _():
            load_out.start()
            load_val.start()

        load_dec.start()
        base = (f * 2 + c) * enc.shape[0]
        wanted = jnp.full((8, 1), -1, jnp.int32)
        for t in range(8):
            wanted = jnp.where(own_row == t, ids_ref[t] - base, wanted)
        hit = lax.broadcasted_iota(jnp.int32, (8, enc.shape[0]), 1) == wanted
        rows[...] = jnp.dot(hit.astype(BF16), enc[...], preferred_element_type=F32)

    def positions(group):
        at = jnp.full((8, 1), -1, jnp.int32)
        for t in range(TGT):
            at = jnp.where(own_row == t, pos_ref[t + TGT * group], at)
        return at

    def top_scores(group):
        at_lane = ((lane_t == row_t) & (lane_p == positions(group))).astype(F32)
        part = lax.dot_general(dec[1], top_own[...].astype(BF16), NT, preferred_element_type=F32)
        score_ref[...] = jnp.dot(part, at_lane, preferred_element_type=F32, precision=lax.Precision.HIGHEST)

    def gather(full, k, sent, use, arrives=True):
        def copy(b, dev, i):
            part = full.at[pl.ds(pl.multiple_of(b * SL, 16), SL)]
            return remote(part, part, g_send.at[k, i], g_recv.at[k, b], dev)

        def start(item):
            item.start()
            sent.append(item)

        def forward(b, i):
            for j, dy in enumerate(Y_ORDER):
                start(copy(b, ydev(dy), 3 * i + j))

        if arrives:
            copy(f, ydev(1), 0).wait_recv()
        forward(f, 0)
        for i, dz in enumerate(Z_ORDER):
            start(copy(f, zdev(dz), 24 + i))
        for i, dz in enumerate(Z_ORDER):
            b = lax.rem(z + NZ - dz, NZ) * NY + y
            copy(b, ydev(1), 0).wait_recv()
            forward(b, 1 + i)
        span = 2 * NY * SL
        for dq in (0, 1, 3, 2):
            q = lax.rem(z // 2 + dq, NZ // 2)
            for half in range(2):
                for dy in Y_ORDER:
                    b = (2 * q + half) * NY + lax.rem(y + dy, NY)
                    copy(b, ydev(1), 0).wait_recv()
            part = pl.ds(pl.multiple_of(q * span, 128), span)
            use(part, full[part, :])

    def add_up(part, block):
        score_ref[...] += jnp.dot(dec[1, :, part], block, preferred_element_type=F32)

    def add_out(part, block):
        score_ref[...] += jnp.dot(dec[0, :, part], block, preferred_element_type=F32)

    def finish(sent):
        for item in sent:
            item.wait_send()

    def attribution_copy(src, full, k, layer, group, i):
        return remote(src, full.at[own], attr_send.at[i], g_recv.at[k, f], (layer, f, group))

    def gin_copy(src, plane, dy, i, j):
        dev = (plane, z * NY + lax.rem(y + dy, NY), 1)
        return remote(src, gin.at[i, gin_own], gin_send.at[j, dy], gin_recv.at[i, y], dev)

    def gin_wait(i, dy):
        j = lax.rem(y + dy, NY)
        part = gin.at[i, pl.ds(pl.multiple_of(PAD + j * SL, 16), SL)]
        remote(part, part, gin_send.at[0, 0], gin_recv.at[i, j], ydev(1)).wait_recv()

    home_slot = jnp.where(s == 0, 1, 0)

    def w_copy(dz, kind):
        zz = lax.rem(z + dz, NZ)
        ss, rs = w_send.at[kind, dz], w_recv.at[kind, z]
        if kind == 0:
            first = pl.multiple_of(zz * BLOCK - PAD * (zz % 2), 128)
            return remote(outp.at[:, pl.ds(first, WIN)], ow.at[home_slot, z], ss, rs, zdev(dz))
        src = val.at[pl.ds(pl.multiple_of(zz * BLOCK, 16), BLOCK)]
        dst = vw.at[home_slot, :, pl.ds(pl.multiple_of(z * HD, 128), HD)]
        return remote(src, dst, ss, rs, zdev(dz))

    def on_copy(kind, di):
        ref = (ow, vw, mixw)[kind].at[home_slot]
        dest = 2 if di == 1 else jnp.where(s == 1, 0, 3)
        return remote(ref, ref, f_send.at[di, kind], f_recv.at[home_slot, kind], (dest, f, 1))

    def piece_copy(zz, di):
        ref = ow.at[home_slot, zz]
        dest = 2 if di == 1 else jnp.where(s == 1, 0, 3)
        return remote(ref, ref, o_send.at[di, zz], o_recv.at[home_slot, zz], (dest, f, 1))

    def piece_start(zz):
        piece_copy(zz, 0).start()

        @pl.when(s == 0)
        def _():
            piece_copy(zz, 1).start()

    def on_start(kind):
        on_copy(kind, 0).start()

        @pl.when(s == 0)
        def _():
            on_copy(kind, 1).start()

    def w_arrived(kind):
        if kind == 0:
            piece_start(z)
        for dz in Z_ORDER:
            zz = lax.rem(z + NZ - dz, NZ)
            if kind == 0:
                part = ow.at[home_slot, zz]
            else:
                part = vw.at[home_slot, :, pl.ds(pl.multiple_of(zz * HD, 128), HD)]
            remote(part, part, w_send.at[kind, 0], w_recv.at[kind, zz], ydev(1)).wait_recv()
            if kind == 0:
                piece_start(zz)

    def weights_start():
        load_out.wait()
        outp[...] = (outp[...].astype(F32) * pgain_ref[...]).astype(BF16)
        for dz in Z_FAR:
            w_copy(dz, 0).start()
        ow[home_slot, z] = outp[:, pl.ds(pl.multiple_of(z * BLOCK - PAD * (z % 2), 128), WIN)]
        scaled = pattern * column(pscale_ref[...]) * qscale_ref[...]
        wide = jnp.concatenate([scaled] * TGT, axis=1)
        wide = jnp.concatenate([wide] * TGT, axis=0)
        same = (lax.broadcasted_iota(jnp.int32, wide.shape, 0) // SEQ
                == lax.broadcasted_iota(jnp.int32, wide.shape, 1) // SEQ)
        mixw[home_slot] = jnp.where(same, wide, 0.0).astype(BF16)
        on_start(2)
        load_val.wait()
        for k in range(FEATS):
            part = slice(k * SL, (k + 1) * SL)
            val[part, :] = (val[part, :].astype(F32) * column(qgain_ref[:, part])).astype(BF16)

        @pl.when(s == 2)
        def _():
            raw_copy().start()

        for dz in Z_FAR:
            w_copy(dz, 1).start()
        vw[home_slot, :, pl.ds(pl.multiple_of(z * HD, 128), HD)] = val[pl.ds(pl.multiple_of(z * BLOCK, 16), BLOCK), :]
        w_arrived(0)

        @pl.when(s < 2)
        def _():
            w_arrived(1)
            on_start(1)

    def raw_copy():
        return remote(val, up, f_send.at[0, 1], f_recv.at[0, 1], (3, f, 1))

    def raw_part(dz):
        zz = lax.rem(z + dz, NZ)
        src = up.at[pl.ds(pl.multiple_of(zz * BLOCK, 16), BLOCK)]
        dst = vw.at[0, :, pl.ds(pl.multiple_of(z * HD, 128), HD)]
        return remote(src, dst, w_send.at[1, dz], w_recv.at[1, z], zdev(dz))

    def raw_start():
        raw_copy().wait_recv()
        for dz in Z_FAR:
            raw_part(dz).start()
        vw[0, :, pl.ds(pl.multiple_of(z * HD, 128), HD)] = up[pl.ds(pl.multiple_of(z * BLOCK, 16), BLOCK), :]

    def raw_done():
        for dz in Z_FAR:
            raw_part(dz).wait_send()

    def weights_done():
        for kind in range(2):
            for dz in Z_FAR:
                w_copy(dz, kind).wait_send()
        @pl.when(s == 2)
        def _():
            raw_copy().wait_send()

        @pl.when(s < 2)
        def _():
            on_copy(1, 0).wait_send()

        on_copy(2, 0).wait_send()

        @pl.when(s == 0)
        def _():
            on_copy(1, 1).wait_send()
            on_copy(2, 1).wait_send()

        for zz in range(NZ):
            piece_copy(zz, 0).wait_send()

            @pl.when(s == 0)
            def _():
                piece_copy(zz, 1).wait_send()

    def w_wait(i, kind):
        def one():
            if kind == 0:
                for zz in range(NZ):
                    ref = ow.at[i, zz]
                    remote(ref, ref, o_send.at[0, 0], o_recv.at[i, zz], ydev(1)).wait_recv()
                return
            ref = (ow, vw, mixw)[kind].at[i]
            remote(ref, ref, f_send.at[0, kind], f_recv.at[i, kind], ydev(1)).wait_recv()

        if i == 1:
            one()
        elif kind != 1:
            pl.when((s == 0) | (s == 3))(one)
        else:
            pl.when(s == 0)(one)

            @pl.when(s >= 2)
            def _():
                for dz in Z_ORDER:
                    zz = lax.rem(z + dz, NZ)
                    part = vw.at[0, :, pl.ds(pl.multiple_of(zz * HD, 128), HD)]
                    remote(part, part, w_send.at[1, 0], w_recv.at[1, zz], ydev(1)).wait_recv()

    def layer_step(i):
        gin[i, 0:PAD] = jnp.zeros((PAD, COLS), BF16)
        gin[i, PAD + BLOCK:] = jnp.zeros((PAD, COLS), BF16)
        w_wait(i, 0)
        w_wait(i, 2)
        for dy in Y_ORDER:
            gin_wait(i, dy)
        if i == 1:
            gin_wait(i, 0)
        else:
            @pl.when(s < 3)
            def _():
                gin_wait(i, 0)

        block = gin[i, pl.ds(pl.multiple_of(PAD * (1 - z % 2), 16), WIN), :]

        def h_copy(dz):
            zz = lax.rem(z + dz, NZ)
            return remote(hsrc.at[i, zz], hpart.at[i, z], h_send.at[i, dz], h_recv.at[i, z], zdev(dz))

        for dz in Z_FAR:
            zz = lax.rem(z + dz, NZ)
            hsrc[i, zz] = jnp.dot(ow[i, zz], block, preferred_element_type=F32).astype(BF16)
            h_copy(dz).start()
        total = jnp.dot(ow[i, z], block, preferred_element_type=F32)
        for dz in Z_ORDER:
            zz = lax.rem(z + dz, NZ)
            remote(hpart.at[i, zz], hpart.at[i, zz], h_send.at[i, 0], h_recv.at[i, zz], ydev(1)).wait_recv()
            total = total + hpart[i, zz].astype(F32)
        mixed = jnp.dot(total.astype(BF16), mixw[i], preferred_element_type=F32).astype(BF16)
        mine = pl.ds(pl.multiple_of(z * HD, 128), HD)
        hm[i, mine, :] = mixed

        def hm_copy(dz):
            return remote(hm.at[i, mine], hm.at[i, mine], m_send.at[i, dz], m_recv.at[i, z], zdev(dz))

        for dz in Z_FAR:
            hm_copy(dz).start()
        w_wait(i, 1)
        for dz in Z_ORDER:
            zz = lax.rem(z + dz, NZ)
            part = hm.at[i, pl.ds(pl.multiple_of(zz * HD, 128), HD)]
            remote(part, part, m_send.at[i, 0], m_recv.at[i, zz], ydev(1)).wait_recv()

        def g_part(dy):
            yy = lax.rem(y + dy, NY)
            weights = vw[i, pl.ds(pl.multiple_of(yy * SL, 16), SL), :]
            return jnp.dot(weights, hm[i], preferred_element_type=F32)

        def gp_copy(dy):
            yy = lax.rem(y + dy, NY)
            return remote(gsrc.at[i, yy], gpart.at[i, y], y_send.at[i, dy], y_recv.at[i, y], ydev(dy))

        for dy in Y_FAR:
            gsrc[i, lax.rem(y + dy, NY)] = g_part(dy).astype(BF16)
            gp_copy(dy).start()
        total = g_part(0) + gin[i, gin_own, :].astype(F32)
        for dy in Y_ORDER:
            yy = lax.rem(y + dy, NY)
            remote(gpart.at[i, yy], gpart.at[i, yy], y_send.at[i, 0], y_recv.at[i, yy], ydev(1)).wait_recv()
            total = total + gpart[i, yy].astype(F32)
        res[i] = total.astype(BF16)

        def done():
            for dz in Z_FAR:
                h_copy(dz).wait_send()
                hm_copy(dz).wait_send()
            for dy in Y_FAR:
                gp_copy(dy).wait_send()

        return done

    def top_layer():
        me = y

        def packed(value):
            rest = jnp.concatenate([value[:, WIN:], jnp.zeros((8, 2 * WIN - QUARTER), F32)], axis=1)
            return jnp.concatenate([value[:, :WIN], rest], axis=0).astype(BF16)

        def unpacked(value):
            value = value.astype(F32)
            return jnp.concatenate([value[:8], value[8:, :QUARTER - WIN]], axis=1)

        def e_copy(stage, src, dst, k, slot, dev):
            return remote(src, dst.at[slot], e_send.at[stage, k], e_recv.at[stage, slot], dev)

        remote(rows0, rows0, core_sem.at[0], core_sem.at[1], (s, f, 0)).wait_recv()
        rows[...] = rows[...] + rows0[...]
        for k in range(NY):
            epack[k] = packed(rows[:, k * QUARTER:(k + 1) * QUARTER])

        def e1_copy(dy):
            return e_copy(0, epack.at[lax.rem(y + dy, NY)], e1, dy, me, ydev(dy))

        for dy in Y_FAR:
            e1_copy(dy).start()
        total = epack[me].astype(F32)
        for dy in Y_ORDER:
            j = lax.rem(y + dy, NY)
            e_copy(0, e2src, e1, 0, j, ydev(1)).wait_recv()
            total = total + e1[j].astype(F32)
        e2src[...] = total.astype(BF16)

        def e2_copy(dz):
            return e_copy(1, e2src, e2, dz, z, zdev(dz))

        for dz in Z_FAR:
            e2_copy(dz).start()
        for dz in Z_ORDER:
            j = lax.rem(z + dz, NZ)
            e_copy(1, e2src, e2, 0, j, ydev(1)).wait_recv()
            total = total + e2[j].astype(F32)
        e3[me] = total.astype(BF16)

        def e3_copy(dy):
            return e_copy(2, e3.at[me], e3, dy, me, ydev(dy))

        for dy in Y_FAR:
            e3_copy(dy).start()
        for dy in Y_ORDER:
            e_copy(2, e2src, e3, 0, lax.rem(y + dy, NY), ydev(1)).wait_recv()
        raw = jnp.concatenate([unpacked(e3[k]) for k in range(NY)], axis=1)

        tops, scaled, at_rows, lanes = [], [], [], []
        pattern4 = jnp.concatenate([pattern] * TGT, axis=1)
        qscale4 = jnp.concatenate([qscale_ref[...]] * TGT, axis=1)
        for group in range(2):
            part = raw if group == 0 else pltpu.roll(raw, TGT, 0)
            part = jnp.where(own_row < TGT, part, 0.0)
            at = positions(group)
            at_pos = lax.broadcasted_iota(jnp.int32, (8, SEQ), 1) == at
            t_scale = jnp.sum(jnp.where(at_pos, jnp.broadcast_to(tscale_ref[...], (8, SEQ)), 0.0),
                              axis=1, keepdims=True)
            p_scale = jnp.sum(jnp.where(at_pos, jnp.broadcast_to(pscale_ref[...], (8, SEQ)), 0.0),
                              axis=1, keepdims=True)
            top = (part * tgain_ref[...] * t_scale).astype(BF16).astype(F32)
            tops.append(top)
            scaled.append(top * pgain_ref[...] * p_scale)
            at_row = jnp.dot(at_pos.astype(BF16), pattern4.astype(BF16), preferred_element_type=F32)
            at_rows.append(jnp.where(lane_t == row_t, at_row * qscale4, 0.0))
            lanes.append(((lane_t == row_t) & (lane_p == at)).astype(BF16))
        rows[...] = tops[0]
        top_copy = remote(rows, top_own, core_sem.at[0], core_sem.at[1], (s, f, 0))
        top_own[...] = tops[1]
        load_out.wait()
        both = jnp.concatenate(scaled, axis=0).astype(BF16)
        head_in = lax.dot_general(both, outp[...], NT, preferred_element_type=F32).astype(BF16)
        load_val.wait()
        gap = jnp.zeros((SEQ - (SL - HD), HD), BF16)

        order = [(dz, dy) for dz in Z_FAR + (0,) for dy in Y_FAR + (0,)]

        def m_copy(k):
            dz, dy = order[k]
            to = lax.rem(z + dz, NZ) * NY + lax.rem(y + dy, NY)
            return remote(msg.at[to], recv.at[f], p_send.at[k], p_recv.at[f], (s, to, 1))

        for k, (dz, dy) in enumerate(order):
            to = lax.rem(z + dz, NZ) * NY + lax.rem(y + dy, NY)
            main = val[pl.ds(pl.multiple_of(to * SL, 16), HD), :]
            tail = val[pl.ds(pl.multiple_of(to * SL + HD, 16), SL - HD), :]
            weights = jnp.concatenate([main] + [tail, gap] * TGT, axis=0)
            got = lax.dot_general(head_in, weights, NT, preferred_element_type=F32)
            parts = []
            for group in range(2):
                part = got[8 * group:8 * group + 8]
                spread = jnp.where(lane_t == (row_t + 1) % TGT, part[:, HD:], 0.0)
                low = pltpu.roll(spread + at_rows[group], TGT, 0)
                parts.append(jnp.where(row_t < TGT, part[:, :HD], low))
            value = jnp.concatenate(parts, axis=0).astype(BF16)
            if k == len(order) - 1:
                recv[f] = value
            else:
                msg[to] = value
                m_copy(k).start()
        top_copy.start()
        raw_start()
        for k in range(FEATS):
            qslice[k] = qgain_ref[:, k * SL:(k + 1) * SL]
        gain = column(qslice[f])
        bases = []
        for group in range(2):
            for k in range(FEATS):
                gslice[k] = tops[group][:, k * SL:(k + 1) * SL]
            bases.append(lax.dot_general(gslice[f].astype(BF16), lanes[group], TN, preferred_element_type=F32))

        def m_wait_one(k, carry):
            j = lax.rem(f + k, FEATS)
            remote(msg.at[0], recv.at[j], p_send.at[0], p_recv.at[j], fdev(1)).wait_recv()
            return carry

        lax.fori_loop(1, FEATS, m_wait_one, 0)
        tail_t = lax.broadcasted_iota(jnp.int32, (SL - HD, COLS), 1) // SEQ
        for group in range(2):
            got = recv[...].astype(F32)[:, 8 * group:8 * group + 8, :].reshape(FEATS * 8, COLS)
            got_row = lax.broadcasted_iota(jnp.int32, got.shape, 0) % 8
            got_t = lax.broadcasted_iota(jnp.int32, got.shape, 1) // SEQ
            low = jnp.where((got_row >= TGT) & (got_t == got_row - TGT), got, 0.0)
            high = pltpu.roll(low, FEATS * 8 - TGT, 0)
            left = got.astype(BF16)
            upper = lax.dot_general(left, high.astype(BF16), TN, preferred_element_type=F32)
            under = lax.dot_general(left, low.astype(BF16), TN, preferred_element_type=F32)
            tail = jnp.zeros((SL - HD, COLS), F32)
            for t in range(TGT):
                start = SEQ * ((t + 1) % TGT)
                tail = tail + jnp.where(tail_t == t, under[start:start + SL - HD, :], 0.0)
            new = bases[group] + jnp.concatenate([upper, tail], axis=0) * gain
            res[2 + group] = new.astype(BF16)
            if group == 0:
                for dy in (2, 1, 3, 0):
                    gin_copy(res.at[2], 2, dy, 0, 0).start()
            else:
                for dy in Y_FAR:
                    gin_copy(res.at[3], 3, dy, 0, 1).start()
                gin[0, gin_own, :] = res[3]
                out[own, :] = res[3]
        notes = [attribution_copy(res.at[2], out, 1, 3, 0, 0), attribution_copy(res.at[2], up, 0, 2, 0, 1),
                 attribution_copy(res.at[3], up, 0, 2, 1, 2)]
        for item in notes:
            item.start()

        def done():
            for dy in Y_FAR:
                e1_copy(dy).wait_send()
                e3_copy(dy).wait_send()
                gin_copy(res.at[3], 3, dy, 0, 1).wait_send()
            for dy in range(NY):
                gin_copy(res.at[2], 2, dy, 0, 0).wait_send()
            for dz in Z_FAR:
                e2_copy(dz).wait_send()
            top_copy.wait_send()
            raw_done()
            for item in notes:
                item.wait_send()

            for k in range(FEATS - 1):
                m_copy(k).wait_send()

        return done

    def release():
        pl.semaphore_signal(go_sem, inc=1, device_id=(s, f, 0), device_id_type=MESH)

    to_plane = 3 - s
    gin_slot = jnp.where(s >= 2, 0, 1)
    layer_now = jnp.where(s >= 2, 2, 1)
    group_now = jnp.where((s == 1) | (s == 2), 0, 1)

    def last_z(dz):
        dev = (0, lax.rem(z + dz, NZ) * NY + y, s - 2)
        dst = out.at[pl.ds(pl.multiple_of(f * SL, 16), SPLIT)]
        return remote(res.at[1, pl.ds(0, SPLIT)], dst, l_send.at[dz], g_recv.at[1, f], dev)

    def last_y(dy):
        dev = (0, z * NY + lax.rem(y + dy, NY), s - 2)
        dst = out.at[pl.ds(pl.multiple_of(f * SL + SPLIT, 16), SL - SPLIT)]
        return remote(res.at[1, pl.ds(SPLIT, SL - SPLIT)], dst, l_send.at[NZ + dy], l_recv.at[f], dev)

    def last_gather(sent):
        def copy(part, b, dev, i):
            if part == 0:
                ref = out.at[pl.ds(pl.multiple_of(b * SL, 16), SPLIT)]
                return remote(ref, ref, g_send.at[1, i], g_recv.at[1, b], dev)
            ref = out.at[pl.ds(pl.multiple_of(b * SL + SPLIT, 16), SL - SPLIT)]
            return remote(ref, ref, l_send.at[i], l_recv.at[b], dev)

        def start(item):
            item.start()
            sent.append(item)

        def relay_y(i, dz):
            b = lax.rem(z + NZ - dz, NZ) * NY + y
            copy(0, b, ydev(1), 0).wait_recv()
            for j, dy in enumerate(Y_FAR):
                start(copy(0, b, ydev(dy), 3 * i + j))

        def relay_z(i, dy):
            b = z * NY + lax.rem(y + dy, NY)
            copy(1, b, ydev(1), 0).wait_recv()
            for j, dz in enumerate(Z_FAR):
                start(copy(1, b, zdev(dz), 7 * i + j))

        zs = (0,) + Z_ORDER
        ys = (0,) + Y_ORDER
        for i in range(NZ):
            if i % 2 == 0:
                relay_z(i // 2, ys[i // 2])
            relay_y(i, zs[i])
        span = 2 * NY * SL
        for dq in (0, 1, 3, 2):
            q = lax.rem(z // 2 + dq, NZ // 2)
            for half in range(2):
                zz = 2 * q + half if dq else jnp.where(half == 0, z, z + 1 - 2 * (z % 2))
                for dy in Y_ORDER:
                    copy(0, zz * NY + lax.rem(y + dy, NY), ydev(1), 0).wait_recv()
                if dq or half:
                    for dy in ys:
                        copy(1, zz * NY + lax.rem(y + dy, NY), ydev(1), 0).wait_recv()
            part = pl.ds(pl.multiple_of(q * span, 128), span)
            add_out(part, out[part, :])

    def send_copies():
        items = [gin_copy(res.at[0], to_plane, dy, gin_slot, 2) for dy in (2, 1, 3, 0)]
        return items + [attribution_copy(res.at[0], out, 1, layer_now, group_now, 3)]

    def up_copy():
        return attribution_copy(res.at[0], up, 0, layer_now - 1, group_now, 4)

    def send_on(i):
        for item in send_copies():
            item.start()

        @pl.when(s > 0)
        def _():
            up_copy().start()

        @pl.when(s == 0)
        def _():
            up[own, :] = res[0]

    def send_done():
        for item in send_copies():
            item.wait_send()

        @pl.when(s > 0)
        def _():
            up_copy().wait_send()

    def out_gather():
        @pl.when(s == 0)
        def _():
            sent = []
            last_gather(sent)
            finish(sent)

        @pl.when(s > 0)
        def _():
            sent = []
            gather(out, 1, sent, add_out)
            finish(sent)

        grad_ref[...] = out[own, :].astype(F32)

    @pl.when(c == 0)
    def _():
        @pl.when(s == 3)
        def _():
            pick_rows()
            pl.semaphore_wait(barrier, 14)
            give = remote(rows, rows0, core_sem.at[0], core_sem.at[1], (s, f, 1))
            give.start()
            load_dec.wait()
            remote(rows, top_own, core_sem.at[0], core_sem.at[1], (s, f, 1)).wait_recv()
            top_scores(0)
            pl.semaphore_wait(go_sem, 1)
            give.wait_send()

        @pl.when(s < 3)
        def _():
            @pl.when(s == 0)
            def _():
                pl.semaphore_wait(barrier, 24)

            @pl.when(s > 0)
            def _():
                pl.semaphore_wait(barrier, 14)

            score_ref[...] = jnp.zeros_like(score_ref)
            load_dec.wait()
            sent = []
            pl.semaphore_wait(go_sem, 1)
            gather(up, 0, sent, add_up)
            pl.semaphore_wait(go_sem, 1)
            finish(sent)

        out_gather()

    @pl.when(c == 1)
    def _():
        @pl.when(s == 3)
        def _():
            pick_rows()
            pl.semaphore_wait(barrier, 26)
            top_done = top_layer()
            load_dec.wait()
            step_done = layer_step(0)
            send_on(0)
            release()
            top_scores(1)
            sent = []
            gather(out, 1, sent, add_out, arrives=False)
            grad_ref[...] = out[own, :].astype(F32)
            top_done()
            step_done()
            finish(sent)

        @pl.when(s < 3)
        def _():
            @pl.when(s == 2)
            def _():
                pl.semaphore_wait(barrier, 36)

            @pl.when(s < 2)
            def _():
                pl.semaphore_wait(barrier, 26)

            weights_start()
            load_dec.start()
            score_ref[...] = jnp.zeros_like(score_ref)
            load_dec.wait()
            step_done = layer_step(0)
            send_on(0)
            release()
            release()
            sent = []

            @pl.when(s > 0)
            def _():
                more = []
                gather(up, 0, more, add_up)
                finish(more)

            @pl.when(s == 0)
            def _():
                more = []
                gather(up, 0, more, add_up, arrives=False)
                finish(more)

            step_done()
            weights_done()

        @pl.when(s >= 2)
        def _():
            step_done = layer_step(1)
            last = [last_z(dz) for dz in Z_FAR + (0,)] + [last_y(dy) for dy in Y_FAR + (0,)]
            for item in last[:7:2] + last[8:11] + last[1:8:2] + last[11:]:
                item.start()
            step_done()
            finish(last)

        @pl.when(s < 3)
        def _():
            out_gather()

        send_done()


def pick_kernel(pos_hbm, count_hbm, ids_hbm, act_hbm, score_ref, grad_ref, out_ref, grad_out_ref,
                pos_ref, count_ref, ids_ref, act_ref, turned, picked, sem):
    pairs = ((pos_hbm, pos_ref), (count_hbm, count_ref), (ids_hbm, ids_ref), (act_hbm, act_ref))
    copies = [pltpu.make_async_copy(src, dst, sem.at[i]) for i, (src, dst) in enumerate(pairs)]
    for item in copies:
        item.start()
    turned[...] = score_ref[...].T
    grad_out_ref[0] = grad_ref[...].T.astype(BF16).reshape(TGT, SEQ, SL)
    for item in copies:
        item.wait()
    slots, width = ids_ref.shape[1], ids_ref.shape[2]
    for b in range(slots):
        at = pos_ref[0, b]
        for t in range(TGT):
            picked[t, b:b + 1, :] = turned[pl.ds(t * SEQ + at, 1), :]
    ids = ids_ref[0]
    live = lax.broadcasted_iota(jnp.int32, (slots, width), 0) < count_ref[0, 0]
    inner = ids % 128
    for t in range(TGT):
        low = jnp.take_along_axis(picked[t, :, :128], inner, axis=1, mode="promise_in_bounds")
        high = jnp.take_along_axis(picked[t, :, 128:], inner, axis=1, mode="promise_in_bounds")
        value = jnp.where(ids < 128, low, high) * act_ref[0]
        out_ref[0, t] = jnp.where(live, value, 0.0)


def body(
    target_ids, target_pos, target_gain, target_scale, encoder, post_gain, post_scale, out_proj, pattern,
    value_proj, pre_gain, pre_scale, decoder, block_ids, block_pos, block_act, block_count,
):
    vmem = pl.BlockSpec(memory_space=pltpu.VMEM)
    hbm = pl.BlockSpec(memory_space=pltpu.HBM)
    dma = pltpu.SemaphoreType.DMA
    shard = encoder.shape[0]
    features = decoder.shape[2]
    scores, grads = pl.pallas_call(
        main_kernel,
        out_shape=(
            jax.ShapeDtypeStruct((features, COLS), F32),
            jax.ShapeDtypeStruct((SL, COLS), F32),
        ),
        in_specs=[hbm] * 13,
        out_specs=(vmem, vmem),
        scratch_shapes=[
            pltpu.SMEM((2 * TGT,), jnp.int32),
            pltpu.SMEM((2 * TGT,), jnp.int32),
            pltpu.VMEM((1, D), F32),
            pltpu.VMEM((1, SEQ), F32),
            pltpu.VMEM((1, D), F32),
            pltpu.VMEM((1, SEQ), F32),
            pltpu.VMEM((1, D), F32),
            pltpu.VMEM((1, SEQ), F32),
            pltpu.VMEM((1, 1, SEQ, SEQ), BF16),
            pltpu.VMEM((shard, D), BF16),
            pltpu.VMEM((HD, D), BF16),
            pltpu.VMEM((D, HD), BF16),
            pltpu.VMEM((2, features, D), BF16),
            pltpu.VMEM((8, D), F32),
            pltpu.VMEM((8, D), F32),
            pltpu.VMEM((8, D), F32),
            pltpu.VMEM((NY, 16, WIN), BF16),
            pltpu.VMEM((NY, 16, WIN), BF16),
            pltpu.VMEM((NZ, 16, WIN), BF16),
            pltpu.VMEM((NY, 16, WIN), BF16),
            pltpu.VMEM((16, WIN), BF16),
            pltpu.VMEM((FEATS, 16, COLS), BF16),
            pltpu.VMEM((FEATS, 16, COLS), BF16),
            pltpu.VMEM((FEATS, 8, SL), F32),
            pltpu.VMEM((FEATS, 1, SL), F32),
            pltpu.VMEM((2, NZ, HD, WIN), BF16),
            pltpu.VMEM((2, BLOCK, NZ * HD), BF16),
            pltpu.VMEM((2, COLS, COLS), BF16),
            pltpu.VMEM((2, BLOCK + 2 * PAD, COLS), BF16),
            pltpu.VMEM((2, NZ, HD, COLS), BF16),
            pltpu.VMEM((2, NZ, HD, COLS), BF16),
            pltpu.VMEM((2, NZ * HD, COLS), BF16),
            pltpu.VMEM((2, NY, SL, COLS), BF16),
            pltpu.VMEM((2, NY, SL, COLS), BF16),
            pltpu.VMEM((4, SL, COLS), BF16),
            pltpu.VMEM((D, COLS), BF16),
            pltpu.VMEM((D, COLS), BF16),
            dma((8,)),
            dma((9,)),
            dma((2,)),
            dma((3, NZ)),
            dma((3, NZ)),
            dma((FEATS,)),
            dma((FEATS,)),
            dma((2, NZ)),
            dma((2, NZ)),
            dma((2, 3)),
            dma((2, 3)),
            dma((2, NZ)),
            dma((2, NZ)),
            dma((3, NY)),
            dma((2, NY)),
            dma((8,)),
            dma((2, NZ)),
            dma((2, NZ)),
            dma((2, NZ)),
            dma((2, NZ)),
            dma((2, NY)),
            dma((2, NY)),
            dma((2, FEATS)),
            dma((2, FEATS)),
            dma((FEATS,)),
            dma((FEATS,)),
            pltpu.SemaphoreType.REGULAR,
        ],
        compiler_params=pltpu.CompilerParams(
            collective_id=1, has_side_effects=True, vmem_limit_bytes=60 * 1024 * 1024
        ),
        name="chain",
    )(
        target_ids, target_pos, target_gain.reshape(1, D), target_scale.reshape(1, SEQ), post_gain, post_scale,
        pre_gain, pre_scale, pattern, encoder, out_proj, value_proj, decoder,
    )
    slots, width = block_ids.shape[1], block_ids.shape[2]
    return pl.pallas_call(
        pick_kernel,
        out_shape=(
            jax.ShapeDtypeStruct((1, TGT, slots, width), F32),
            jax.ShapeDtypeStruct((1, TGT, SEQ, SL), BF16),
        ),
        in_specs=[hbm] * 4 + [vmem] * 2,
        out_specs=(vmem, vmem),
        scratch_shapes=[
            pltpu.SMEM((1, slots), jnp.int32),
            pltpu.SMEM((1, 1), jnp.int32),
            pltpu.VMEM((1, slots, width), jnp.int32),
            pltpu.VMEM((1, slots, width), F32),
            pltpu.VMEM((COLS, features), F32),
            pltpu.VMEM((TGT, slots, features), F32),
            dma((4,)),
        ],
        name="pick",
    )(block_pos, block_count, block_ids, block_act, scores, grads)


def solution(mesh):
    in_specs = (
        P(),
        P(),
        P(),
        P(),
        P(("feat", "row"), None),
        P("section", None),
        P("section", None),
        P("section", "feat", None, None),
        P("section", "feat", None, None),
        P("section", "feat", None, None),
        P("section", None),
        P("section", None),
        P("section", None, "feat", None),
        P("section", "feat", None),
        P("section", "feat"),
        P("section", "feat", None),
        P("section", "feat"),
    )
    out_specs = (P("section", "row", "feat", None), P("section", "row", None, "feat"))
    return jax.shard_map(body, mesh=mesh, in_specs=in_specs, out_specs=out_specs, check_vma=False)
```

```python
import functools

import jax
import jax.numpy as jnp
from jax import lax
from jax.experimental import pallas as pl
from jax.experimental.pallas import tpu as pltpu
from jax.sharding import PartitionSpec as P

MESH = pl.DeviceIdType.MESH
F32 = jnp.float32
BF16 = jnp.bfloat16
NT = (((1,), (1,)), ((), ()))
TN = (((0,), (0,)), ((), ()))

D, HD, SEQ, FEATS, TGT = 4608, 128, 32, 32, 4
NZ, NY = 8, 4
SL = D // FEATS
COLS = TGT * SEQ
QUARTER = D // NY
BLOCK = D // NZ
WIN = 640
PAD = WIN - BLOCK
SPLIT = 96
GROUP = 32
Z_ORDER = (1, 7, 2, 6, 3, 5, 4)
Z_FAR = (4, 3, 5, 2, 6, 1, 7)
Y_ORDER = (1, 3, 2)
Y_FAR = (2, 1, 3)


def main_kernel(
    ids_hbm, pos_hbm, tgain_hbm, tscale_hbm, pgain_hbm, pscale_hbm, qgain_hbm, qscale_hbm, pattern_hbm,
    enc_hbm, out_hbm, val_hbm, dec_hbm,
    score_ref, grad_ref,
    ids_ref, pos_ref, tgain_ref, tscale_ref, pgain_ref, pscale_ref, qgain_ref, qscale_ref, pattern_ref,
    enc, outp, val, dec, rows, rows0, top_own, epack, e1, e2, e3, e2src, msg, recv, gslice, qslice,
    ow, vw, mixw, gin, hsrc, hpart, hm, gsrc, gpart, res, up, out,
    load_sem, small_sem, core_sem, e_send, e_recv, p_send, p_recv, w_send, w_recv, f_send, f_recv, o_send, o_recv,
    gin_send, gin_recv, attr_send, h_send, h_recv, m_send, m_recv, y_send, y_recv, g_send, g_recv, l_send, l_recv, go_sem,
):
    s = lax.axis_index("section")
    f = lax.axis_index("feat")
    c = lax.axis_index("row")
    z = f // NY
    y = f % NY

    def zdev(dz):
        return (s, lax.rem(z + dz, NZ) * NY + y, c)

    def ydev(dy):
        return (s, z * NY + lax.rem(y + dy, NY), c)

    def fdev(k):
        return (s, lax.rem(f + k, FEATS), c)

    def remote(src, dst, ss, rs, dev):
        return pltpu.make_async_remote_copy(
            src_ref=src, dst_ref=dst, send_sem=ss, recv_sem=rs, device_id=dev, device_id_type=MESH
        )

    enc_part = enc.shape[0] // 4
    load_enc = [
        pltpu.make_async_copy(enc_hbm.at[pl.ds(k * enc_part, enc_part)], enc.at[pl.ds(k * enc_part, enc_part)],
                              load_sem.at[4 + k])
        for k in range(4)
    ]
    load_out = pltpu.make_async_copy(out_hbm.at[0, 0], outp, load_sem.at[1])
    load_val = pltpu.make_async_copy(val_hbm.at[0, 0], val, load_sem.at[2])
    load_dec = pltpu.make_async_copy(dec_hbm.at[0], dec, load_sem.at[3])
    small = ((ids_hbm, ids_ref), (pos_hbm, pos_ref), (tgain_hbm, tgain_ref), (tscale_hbm, tscale_ref),
             (pgain_hbm, pgain_ref), (pscale_hbm, pscale_ref), (qgain_hbm, qgain_ref), (qscale_hbm, qscale_ref),
             (pattern_hbm, pattern_ref))
    small = [pltpu.make_async_copy(src, dst, small_sem.at[i]) for i, (src, dst) in enumerate(small)]

    @pl.when(s == 3)
    def _():
        for item in load_enc:
            item.start()

    barrier = pltpu.get_barrier_semaphore()

    def hello(dev):
        pl.semaphore_signal(barrier, inc=1, device_id=dev, device_id_type=MESH)

    for dz in Z_FAR:
        hello(zdev(dz))
    for dy in Y_FAR:
        hello(ydev(dy))

    def column_peers(plane, core):
        for dz in Z_FAR:
            hello((plane, lax.rem(z + dz, NZ) * NY + y, core))

    def row_peers(plane, core):
        for dy in Y_FAR:
            hello((plane, z * NY + lax.rem(y + dy, NY), core))

    @pl.when((c == 0) & (s == 0))
    def _():
        column_peers(2, 1)
        row_peers(2, 1)

    @pl.when(c == 1)
    def _():
        @pl.when(s == 2)
        def _():
            column_peers(0, 0)
            row_peers(0, 0)

        for k in (2, 1, 3):
            q = lax.rem(s + k, 4)
            row_peers(q, 1)
            hello((q, f, 1))

    for q in range(4):
        hello((q, f, 1 - c))

    for item in small:
        item.start()

    @pl.when((s < 3) & (c == 1))
    def _():
        load_out.start()
        load_val.start()

    @pl.when((s < 3) & (c == 0))
    def _():
        load_dec.start()

    for item in small:
        item.wait()

    lane_t = lax.broadcasted_iota(jnp.int32, (8, COLS), 1) // SEQ
    lane_p = lax.broadcasted_iota(jnp.int32, (8, COLS), 1) % SEQ
    row_t = lax.broadcasted_iota(jnp.int32, (8, COLS), 0)
    own_row = lax.broadcasted_iota(jnp.int32, (8, 1), 0)
    own = pl.ds(pl.multiple_of(f * SL, 16), SL)
    gin_own = pl.ds(pl.multiple_of(PAD + y * SL, 16), SL)
    pattern = pattern_ref[0, 0].astype(F32)

    def column(row):
        n = row.shape[1]
        eye = lax.broadcasted_iota(jnp.int32, (n, n), 0) == lax.broadcasted_iota(jnp.int32, (n, n), 1)
        return jnp.sum(jnp.where(eye, jnp.broadcast_to(row, (n, n)), 0.0), axis=1, keepdims=True)

    def pick_rows():
        for item in load_enc:
            item.wait()

        @pl.when(c == 1)
        def _():
            load_out.start()
            load_val.start()

        load_dec.start()
        base = (f * 2 + c) * enc.shape[0]
        wanted = jnp.full((8, 1), -1, jnp.int32)
        for t in range(8):
            wanted = jnp.where(own_row == t, ids_ref[t] - base, wanted)
        hit = lax.broadcasted_iota(jnp.int32, (8, enc.shape[0]), 1) == wanted
        rows[...] = jnp.dot(hit.astype(BF16), enc[...], preferred_element_type=F32)

    def positions(group):
        at = jnp.full((8, 1), -1, jnp.int32)
        for t in range(TGT):
            at = jnp.where(own_row == t, pos_ref[t + TGT * group], at)
        return at

    def top_scores(group):
        at_lane = ((lane_t == row_t) & (lane_p == positions(group))).astype(F32)
        part = lax.dot_general(dec[1], top_own[...].astype(BF16), NT, preferred_element_type=F32)
        score_ref[...] = jnp.dot(part, at_lane, preferred_element_type=F32, precision=lax.Precision.HIGHEST)

    def gather(full, k, sent, use, arrives=True):
        def copy(b, dev, i):
            part = full.at[pl.ds(pl.multiple_of(b * SL, 16), SL)]
            return remote(part, part, g_send.at[k, i], g_recv.at[k, b], dev)

        def start(item):
            item.start()
            sent.append(item)

        def forward(b, i):
            for j, dy in enumerate(Y_ORDER):
                start(copy(b, ydev(dy), 3 * i + j))

        if arrives:
            copy(f, ydev(1), 0).wait_recv()
        forward(f, 0)
        for i, dz in enumerate(Z_ORDER):
            start(copy(f, zdev(dz), 24 + i))
        for i, dz in enumerate(Z_ORDER):
            b = lax.rem(z + NZ - dz, NZ) * NY + y
            copy(b, ydev(1), 0).wait_recv()
            forward(b, 1 + i)
        span = 2 * NY * SL
        for dq in (0, 1, 3, 2):
            q = lax.rem(z // 2 + dq, NZ // 2)
            for half in range(2):
                for dy in Y_ORDER:
                    b = (2 * q + half) * NY + lax.rem(y + dy, NY)
                    copy(b, ydev(1), 0).wait_recv()
            part = pl.ds(pl.multiple_of(q * span, 128), span)
            use(part, full[part, :])

    def add_up(part, block):
        score_ref[...] += jnp.dot(dec[1, :, part], block, preferred_element_type=F32)

    def add_out(part, block):
        score_ref[...] += jnp.dot(dec[0, :, part], block, preferred_element_type=F32)

    def finish(sent):
        for item in sent:
            item.wait_send()

    def attribution_copy(src, full, k, layer, group, i):
        return remote(src, full.at[own], attr_send.at[i], g_recv.at[k, f], (layer, f, group))

    def gin_copy(src, plane, dy, i, j):
        dev = (plane, z * NY + lax.rem(y + dy, NY), 1)
        return remote(src, gin.at[i, gin_own], gin_send.at[j, dy], gin_recv.at[i, y], dev)

    def gin_wait(i, dy):
        j = lax.rem(y + dy, NY)
        part = gin.at[i, pl.ds(pl.multiple_of(PAD + j * SL, 16), SL)]
        remote(part, part, gin_send.at[0, 0], gin_recv.at[i, j], ydev(1)).wait_recv()

    home_slot = jnp.where(s == 0, 1, 0)

    def w_copy(dz, kind):
        zz = lax.rem(z + dz, NZ)
        ss, rs = w_send.at[kind, dz], w_recv.at[kind, z]
        if kind == 0:
            first = pl.multiple_of(zz * BLOCK - PAD * (zz % 2), 128)
            return remote(outp.at[:, pl.ds(first, WIN)], ow.at[home_slot, z], ss, rs, zdev(dz))
        src = val.at[pl.ds(pl.multiple_of(zz * BLOCK, 16), BLOCK)]
        dst = vw.at[home_slot, :, pl.ds(pl.multiple_of(z * HD, 128), HD)]
        return remote(src, dst, ss, rs, zdev(dz))

    def on_copy(kind, di):
        ref = (ow, vw, mixw)[kind].at[home_slot]
        dest = 2 if di == 1 else jnp.where(s == 1, 0, 3)
        return remote(ref, ref, f_send.at[di, kind], f_recv.at[home_slot, kind], (dest, f, 1))

    def piece_copy(zz, di):
        ref = ow.at[home_slot, zz]
        dest = 2 if di == 1 else jnp.where(s == 1, 0, 3)
        return remote(ref, ref, o_send.at[di, zz], o_recv.at[home_slot, zz], (dest, f, 1))

    def piece_start(zz):
        piece_copy(zz, 0).start()

        @pl.when(s == 0)
        def _():
            piece_copy(zz, 1).start()

    def on_start(kind):
        on_copy(kind, 0).start()

        @pl.when(s == 0)
        def _():
            on_copy(kind, 1).start()

    def w_arrived(kind):
        if kind == 0:
            piece_start(z)
        for dz in Z_ORDER:
            zz = lax.rem(z + NZ - dz, NZ)
            if kind == 0:
                part = ow.at[home_slot, zz]
            else:
                part = vw.at[home_slot, :, pl.ds(pl.multiple_of(zz * HD, 128), HD)]
            remote(part, part, w_send.at[kind, 0], w_recv.at[kind, zz], ydev(1)).wait_recv()
            if kind == 0:
                piece_start(zz)

    def weights_start():
        load_out.wait()
        outp[...] = (outp[...].astype(F32) * pgain_ref[...]).astype(BF16)
        for dz in Z_FAR:
            w_copy(dz, 0).start()
        ow[home_slot, z] = outp[:, pl.ds(pl.multiple_of(z * BLOCK - PAD * (z % 2), 128), WIN)]
        scaled = pattern * column(pscale_ref[...]) * qscale_ref[...]
        wide = jnp.concatenate([scaled] * TGT, axis=1)
        wide = jnp.concatenate([wide] * TGT, axis=0)
        same = (lax.broadcasted_iota(jnp.int32, wide.shape, 0) // SEQ
                == lax.broadcasted_iota(jnp.int32, wide.shape, 1) // SEQ)
        mixw[home_slot] = jnp.where(same, wide, 0.0).astype(BF16)
        on_start(2)
        load_val.wait()
        for k in range(FEATS):
            part = slice(k * SL, (k + 1) * SL)
            val[part, :] = (val[part, :].astype(F32) * column(qgain_ref[:, part])).astype(BF16)

        @pl.when(s == 2)
        def _():
            raw_copy().start()

        for dz in Z_FAR:
            w_copy(dz, 1).start()
        vw[home_slot, :, pl.ds(pl.multiple_of(z * HD, 128), HD)] = val[pl.ds(pl.multiple_of(z * BLOCK, 16), BLOCK), :]
        w_arrived(0)

        @pl.when(s < 2)
        def _():
            w_arrived(1)
            on_start(1)

    def raw_copy():
        return remote(val, up, f_send.at[0, 1], f_recv.at[0, 1], (3, f, 1))

    def raw_part(dz):
        zz = lax.rem(z + dz, NZ)
        src = up.at[pl.ds(pl.multiple_of(zz * BLOCK, 16), BLOCK)]
        dst = vw.at[0, :, pl.ds(pl.multiple_of(z * HD, 128), HD)]
        return remote(src, dst, w_send.at[1, dz], w_recv.at[1, z], zdev(dz))

    def raw_start():
        raw_copy().wait_recv()
        for dz in Z_FAR:
            raw_part(dz).start()
        vw[0, :, pl.ds(pl.multiple_of(z * HD, 128), HD)] = up[pl.ds(pl.multiple_of(z * BLOCK, 16), BLOCK), :]

    def raw_done():
        for dz in Z_FAR:
            raw_part(dz).wait_send()

    def weights_done():
        for kind in range(2):
            for dz in Z_FAR:
                w_copy(dz, kind).wait_send()
        @pl.when(s == 2)
        def _():
            raw_copy().wait_send()

        @pl.when(s < 2)
        def _():
            on_copy(1, 0).wait_send()

        on_copy(2, 0).wait_send()

        @pl.when(s == 0)
        def _():
            on_copy(1, 1).wait_send()
            on_copy(2, 1).wait_send()

        for zz in range(NZ):
            piece_copy(zz, 0).wait_send()

            @pl.when(s == 0)
            def _():
                piece_copy(zz, 1).wait_send()

    def w_wait(i, kind):
        def one():
            if kind == 0:
                for zz in range(NZ):
                    ref = ow.at[i, zz]
                    remote(ref, ref, o_send.at[0, 0], o_recv.at[i, zz], ydev(1)).wait_recv()
                return
            ref = (ow, vw, mixw)[kind].at[i]
            remote(ref, ref, f_send.at[0, kind], f_recv.at[i, kind], ydev(1)).wait_recv()

        if i == 1:
            one()
        elif kind != 1:
            pl.when((s == 0) | (s == 3))(one)
        else:
            pl.when(s == 0)(one)

            @pl.when(s >= 2)
            def _():
                for dz in Z_ORDER:
                    zz = lax.rem(z + dz, NZ)
                    part = vw.at[0, :, pl.ds(pl.multiple_of(zz * HD, 128), HD)]
                    remote(part, part, w_send.at[1, 0], w_recv.at[1, zz], ydev(1)).wait_recv()

    def layer_step(i):
        gin[i, 0:PAD] = jnp.zeros((PAD, COLS), BF16)
        gin[i, PAD + BLOCK:] = jnp.zeros((PAD, COLS), BF16)
        w_wait(i, 0)
        w_wait(i, 2)
        for dy in Y_ORDER:
            gin_wait(i, dy)
        if i == 1:
            gin_wait(i, 0)
        else:
            @pl.when(s < 3)
            def _():
                gin_wait(i, 0)

        block = gin[i, pl.ds(pl.multiple_of(PAD * (1 - z % 2), 16), WIN), :]

        def h_copy(dz):
            zz = lax.rem(z + dz, NZ)
            return remote(hsrc.at[i, zz], hpart.at[i, z], h_send.at[i, dz], h_recv.at[i, z], zdev(dz))

        for dz in Z_FAR:
            zz = lax.rem(z + dz, NZ)
            hsrc[i, zz] = jnp.dot(ow[i, zz], block, preferred_element_type=F32).astype(BF16)
            h_copy(dz).start()
        total = jnp.dot(ow[i, z], block, preferred_element_type=F32)
        for dz in Z_ORDER:
            zz = lax.rem(z + dz, NZ)
            remote(hpart.at[i, zz], hpart.at[i, zz], h_send.at[i, 0], h_recv.at[i, zz], ydev(1)).wait_recv()
            total = total + hpart[i, zz].astype(F32)
        mixed = jnp.dot(total.astype(BF16), mixw[i], preferred_element_type=F32).astype(BF16)
        mine = pl.ds(pl.multiple_of(z * HD, 128), HD)
        hm[i, mine, :] = mixed

        def hm_copy(dz):
            return remote(hm.at[i, mine], hm.at[i, mine], m_send.at[i, dz], m_recv.at[i, z], zdev(dz))

        for dz in Z_FAR:
            hm_copy(dz).start()
        w_wait(i, 1)
        for dz in Z_ORDER:
            zz = lax.rem(z + dz, NZ)
            part = hm.at[i, pl.ds(pl.multiple_of(zz * HD, 128), HD)]
            remote(part, part, m_send.at[i, 0], m_recv.at[i, zz], ydev(1)).wait_recv()

        def g_part(dy):
            yy = lax.rem(y + dy, NY)
            weights = vw[i, pl.ds(pl.multiple_of(yy * SL, 16), SL), :]
            return jnp.dot(weights, hm[i], preferred_element_type=F32)

        def gp_copy(dy):
            yy = lax.rem(y + dy, NY)
            return remote(gsrc.at[i, yy], gpart.at[i, y], y_send.at[i, dy], y_recv.at[i, y], ydev(dy))

        for dy in Y_FAR:
            gsrc[i, lax.rem(y + dy, NY)] = g_part(dy).astype(BF16)
            gp_copy(dy).start()
        total = g_part(0) + gin[i, gin_own, :].astype(F32)
        for dy in Y_ORDER:
            yy = lax.rem(y + dy, NY)
            remote(gpart.at[i, yy], gpart.at[i, yy], y_send.at[i, 0], y_recv.at[i, yy], ydev(1)).wait_recv()
            total = total + gpart[i, yy].astype(F32)
        res[i] = total.astype(BF16)

        def done():
            for dz in Z_FAR:
                h_copy(dz).wait_send()
                hm_copy(dz).wait_send()
            for dy in Y_FAR:
                gp_copy(dy).wait_send()

        return done

    def top_layer():
        me = y

        def packed(value):
            rest = jnp.concatenate([value[:, WIN:], jnp.zeros((8, 2 * WIN - QUARTER), F32)], axis=1)
            return jnp.concatenate([value[:, :WIN], rest], axis=0).astype(BF16)

        def unpacked(value):
            value = value.astype(F32)
            return jnp.concatenate([value[:8], value[8:, :QUARTER - WIN]], axis=1)

        def e_copy(stage, src, dst, k, slot, dev):
            return remote(src, dst.at[slot], e_send.at[stage, k], e_recv.at[stage, slot], dev)

        remote(rows0, rows0, core_sem.at[0], core_sem.at[1], (s, f, 0)).wait_recv()
        rows[...] = rows[...] + rows0[...]
        for k in range(NY):
            epack[k] = packed(rows[:, k * QUARTER:(k + 1) * QUARTER])

        def e1_copy(dy):
            return e_copy(0, epack.at[lax.rem(y + dy, NY)], e1, dy, me, ydev(dy))

        for dy in Y_FAR:
            e1_copy(dy).start()
        total = epack[me].astype(F32)
        for dy in Y_ORDER:
            j = lax.rem(y + dy, NY)
            e_copy(0, e2src, e1, 0, j, ydev(1)).wait_recv()
            total = total + e1[j].astype(F32)
        e2src[...] = total.astype(BF16)

        def e2_copy(dz):
            return e_copy(1, e2src, e2, dz, z, zdev(dz))

        for dz in Z_FAR:
            e2_copy(dz).start()
        for dz in Z_ORDER:
            j = lax.rem(z + dz, NZ)
            e_copy(1, e2src, e2, 0, j, ydev(1)).wait_recv()
            total = total + e2[j].astype(F32)
        e3[me] = total.astype(BF16)

        def e3_copy(dy):
            return e_copy(2, e3.at[me], e3, dy, me, ydev(dy))

        for dy in Y_FAR:
            e3_copy(dy).start()
        for dy in Y_ORDER:
            e_copy(2, e2src, e3, 0, lax.rem(y + dy, NY), ydev(1)).wait_recv()
        raw = jnp.concatenate([unpacked(e3[k]) for k in range(NY)], axis=1)

        tops, scaled, at_rows, lanes = [], [], [], []
        pattern4 = jnp.concatenate([pattern] * TGT, axis=1)
        qscale4 = jnp.concatenate([qscale_ref[...]] * TGT, axis=1)
        for group in range(2):
            part = raw if group == 0 else pltpu.roll(raw, TGT, 0)
            part = jnp.where(own_row < TGT, part, 0.0)
            at = positions(group)
            at_pos = lax.broadcasted_iota(jnp.int32, (8, SEQ), 1) == at
            t_scale = jnp.sum(jnp.where(at_pos, jnp.broadcast_to(tscale_ref[...], (8, SEQ)), 0.0),
                              axis=1, keepdims=True)
            p_scale = jnp.sum(jnp.where(at_pos, jnp.broadcast_to(pscale_ref[...], (8, SEQ)), 0.0),
                              axis=1, keepdims=True)
            top = (part * tgain_ref[...].reshape(1, D) * t_scale).astype(BF16).astype(F32)
            tops.append(top)
            scaled.append(top * pgain_ref[...] * p_scale)
            at_row = jnp.dot(at_pos.astype(BF16), pattern4.astype(BF16), preferred_element_type=F32)
            at_rows.append(jnp.where(lane_t == row_t, at_row * qscale4, 0.0))
            lanes.append(((lane_t == row_t) & (lane_p == at)).astype(BF16))
        rows[...] = tops[0]
        top_copy = remote(rows, top_own, core_sem.at[0], core_sem.at[1], (s, f, 0))
        top_own[...] = tops[1]
        load_out.wait()
        both = jnp.concatenate(scaled, axis=0).astype(BF16)
        head_in = lax.dot_general(both, outp[...], NT, preferred_element_type=F32).astype(BF16)
        load_val.wait()
        gap = jnp.zeros((SEQ - (SL - HD), HD), BF16)

        order = [(dz, dy) for dz in Z_FAR + (0,) for dy in Y_FAR + (0,)]

        def m_copy(k):
            dz, dy = order[k]
            to = lax.rem(z + dz, NZ) * NY + lax.rem(y + dy, NY)
            return remote(msg.at[to], recv.at[f], p_send.at[k], p_recv.at[f], (s, to, 1))

        for k, (dz, dy) in enumerate(order):
            if k % GROUP == 0:
                for e in range(max(k - GROUP, 0), k):
                    m_copy(e).start()
            to = lax.rem(z + dz, NZ) * NY + lax.rem(y + dy, NY)
            main = val[pl.ds(pl.multiple_of(to * SL, 16), HD), :]
            tail = val[pl.ds(pl.multiple_of(to * SL + HD, 16), SL - HD), :]
            weights = jnp.concatenate([main] + [tail, gap] * TGT, axis=0)
            got = lax.dot_general(head_in, weights, NT, preferred_element_type=F32)
            parts = []
            for group in range(2):
                part = got[8 * group:8 * group + 8]
                spread = jnp.where(lane_t == (row_t + 1) % TGT, part[:, HD:], 0.0)
                low = pltpu.roll(spread + at_rows[group], TGT, 0)
                parts.append(jnp.where(row_t < TGT, part[:, :HD], low))
            value = jnp.concatenate(parts, axis=0).astype(BF16)
            if k == len(order) - 1:
                recv[f] = value
            else:
                msg[to] = value
        for e in range((FEATS - 1) // GROUP * GROUP, FEATS - 1):
            m_copy(e).start()
        top_copy.start()
        raw_start()
        for k in range(FEATS):
            qslice[k] = qgain_ref[:, k * SL:(k + 1) * SL]
        gain = column(qslice[f])
        bases = []
        for group in range(2):
            for k in range(FEATS):
                gslice[k] = tops[group][:, k * SL:(k + 1) * SL]
            bases.append(lax.dot_general(gslice[f].astype(BF16), lanes[group], TN, preferred_element_type=F32))

        def m_wait_one(k, carry):
            j = lax.rem(f + k, FEATS)
            remote(msg.at[0], recv.at[j], p_send.at[0], p_recv.at[j], fdev(1)).wait_recv()
            return carry

        lax.fori_loop(1, FEATS, m_wait_one, 0)
        tail_t = lax.broadcasted_iota(jnp.int32, (SL - HD, COLS), 1) // SEQ
        for group in range(2):
            got = recv[...].astype(F32)[:, 8 * group:8 * group + 8, :].reshape(FEATS * 8, COLS)
            got_row = lax.broadcasted_iota(jnp.int32, got.shape, 0) % 8
            got_t = lax.broadcasted_iota(jnp.int32, got.shape, 1) // SEQ
            low = jnp.where((got_row >= TGT) & (got_t == got_row - TGT), got, 0.0)
            high = pltpu.roll(low, FEATS * 8 - TGT, 0)
            left = got.astype(BF16)
            upper = lax.dot_general(left, high.astype(BF16), TN, preferred_element_type=F32)
            under = lax.dot_general(left, low.astype(BF16), TN, preferred_element_type=F32)
            tail = jnp.zeros((SL - HD, COLS), F32)
            for t in range(TGT):
                start = SEQ * ((t + 1) % TGT)
                tail = tail + jnp.where(tail_t == t, under[start:start + SL - HD, :], 0.0)
            new = bases[group] + jnp.concatenate([upper, tail], axis=0) * gain
            res[2 + group] = new.astype(BF16)
            if group == 0:
                for dy in (2, 1, 3, 0):
                    gin_copy(res.at[2], 2, dy, 0, 0).start()
            else:
                for dy in Y_FAR:
                    gin_copy(res.at[3], 3, dy, 0, 1).start()
                gin[0, gin_own, :] = res[3]
                out[own, :] = res[3]
        notes = [attribution_copy(res.at[2], out, 1, 3, 0, 0), attribution_copy(res.at[2], up, 0, 2, 0, 1),
                 attribution_copy(res.at[3], up, 0, 2, 1, 2)]
        for item in notes:
            item.start()

        def done():
            for dy in Y_FAR:
                e1_copy(dy).wait_send()
                e3_copy(dy).wait_send()
                gin_copy(res.at[3], 3, dy, 0, 1).wait_send()
            for dy in range(NY):
                gin_copy(res.at[2], 2, dy, 0, 0).wait_send()
            for dz in Z_FAR:
                e2_copy(dz).wait_send()
            top_copy.wait_send()
            raw_done()
            for item in notes:
                item.wait_send()

            for k in range(FEATS - 1):
                m_copy(k).wait_send()

        return done

    def release():
        pl.semaphore_signal(go_sem, inc=1, device_id=(s, f, 0), device_id_type=MESH)

    to_plane = 3 - s
    gin_slot = jnp.where(s >= 2, 0, 1)
    layer_now = jnp.where(s >= 2, 2, 1)
    group_now = jnp.where((s == 1) | (s == 2), 0, 1)

    def last_z(dz):
        dev = (0, lax.rem(z + dz, NZ) * NY + y, s - 2)
        dst = out.at[pl.ds(pl.multiple_of(f * SL, 16), SPLIT)]
        return remote(res.at[1, pl.ds(0, SPLIT)], dst, l_send.at[dz], g_recv.at[1, f], dev)

    def last_y(dy):
        dev = (0, z * NY + lax.rem(y + dy, NY), s - 2)
        dst = out.at[pl.ds(pl.multiple_of(f * SL + SPLIT, 16), SL - SPLIT)]
        return remote(res.at[1, pl.ds(SPLIT, SL - SPLIT)], dst, l_send.at[NZ + dy], l_recv.at[f], dev)

    def last_gather(sent):
        def copy(part, b, dev, i):
            if part == 0:
                ref = out.at[pl.ds(pl.multiple_of(b * SL, 16), SPLIT)]
                return remote(ref, ref, g_send.at[1, i], g_recv.at[1, b], dev)
            ref = out.at[pl.ds(pl.multiple_of(b * SL + SPLIT, 16), SL - SPLIT)]
            return remote(ref, ref, l_send.at[i], l_recv.at[b], dev)

        def start(item):
            item.start()
            sent.append(item)

        def relay_y(i, dz):
            b = lax.rem(z + NZ - dz, NZ) * NY + y
            copy(0, b, ydev(1), 0).wait_recv()
            for j, dy in enumerate(Y_FAR):
                start(copy(0, b, ydev(dy), 3 * i + j))

        def relay_z(i, dy):
            b = z * NY + lax.rem(y + dy, NY)
            copy(1, b, ydev(1), 0).wait_recv()
            for j, dz in enumerate(Z_FAR):
                start(copy(1, b, zdev(dz), 7 * i + j))

        zs = (0,) + Z_ORDER
        ys = (0,) + Y_ORDER
        for i in range(NZ):
            if i % 2 == 0:
                relay_z(i // 2, ys[i // 2])
            relay_y(i, zs[i])
        span = 2 * NY * SL
        for dq in (0, 1, 3, 2):
            q = lax.rem(z // 2 + dq, NZ // 2)
            for half in range(2):
                zz = 2 * q + half if dq else jnp.where(half == 0, z, z + 1 - 2 * (z % 2))
                for dy in Y_ORDER:
                    copy(0, zz * NY + lax.rem(y + dy, NY), ydev(1), 0).wait_recv()
                if dq or half:
                    for dy in ys:
                        copy(1, zz * NY + lax.rem(y + dy, NY), ydev(1), 0).wait_recv()
            part = pl.ds(pl.multiple_of(q * span, 128), span)
            add_out(part, out[part, :])

    def send_copies():
        items = [gin_copy(res.at[0], to_plane, dy, gin_slot, 2) for dy in (2, 1, 3, 0)]
        return items + [attribution_copy(res.at[0], out, 1, layer_now, group_now, 3)]

    def up_copy():
        return attribution_copy(res.at[0], up, 0, layer_now - 1, group_now, 4)

    def send_on(i):
        for item in send_copies():
            item.start()

        @pl.when(s > 0)
        def _():
            up_copy().start()

        @pl.when(s == 0)
        def _():
            up[own, :] = res[0]

    def send_done():
        for item in send_copies():
            item.wait_send()

        @pl.when(s > 0)
        def _():
            up_copy().wait_send()

    def out_gather():
        @pl.when(s == 0)
        def _():
            sent = []
            last_gather(sent)
            finish(sent)

        @pl.when(s > 0)
        def _():
            sent = []
            gather(out, 1, sent, add_out)
            finish(sent)

        grad_ref[...] = out[own, :].astype(F32)

    @pl.when(c == 0)
    def _():
        @pl.when(s == 3)
        def _():
            pick_rows()
            pl.semaphore_wait(barrier, 14)
            give = remote(rows, rows0, core_sem.at[0], core_sem.at[1], (s, f, 1))
            give.start()
            load_dec.wait()
            remote(rows, top_own, core_sem.at[0], core_sem.at[1], (s, f, 1)).wait_recv()
            top_scores(0)
            pl.semaphore_wait(go_sem, 1)
            give.wait_send()

        @pl.when(s < 3)
        def _():
            @pl.when(s == 0)
            def _():
                pl.semaphore_wait(barrier, 24)

            @pl.when(s > 0)
            def _():
                pl.semaphore_wait(barrier, 14)

            score_ref[...] = jnp.zeros_like(score_ref)
            load_dec.wait()
            sent = []
            pl.semaphore_wait(go_sem, 1)
            gather(up, 0, sent, add_up)
            pl.semaphore_wait(go_sem, 1)
            finish(sent)

        out_gather()

    @pl.when(c == 1)
    def _():
        @pl.when(s == 3)
        def _():
            pick_rows()
            pl.semaphore_wait(barrier, 26)
            top_done = top_layer()
            load_dec.wait()
            step_done = layer_step(0)
            send_on(0)
            release()
            top_scores(1)
            sent = []
            gather(out, 1, sent, add_out, arrives=False)
            grad_ref[...] = out[own, :].astype(F32)
            top_done()
            step_done()
            finish(sent)

        @pl.when(s < 3)
        def _():
            @pl.when(s == 2)
            def _():
                pl.semaphore_wait(barrier, 36)

            @pl.when(s < 2)
            def _():
                pl.semaphore_wait(barrier, 26)

            weights_start()
            load_dec.start()
            score_ref[...] = jnp.zeros_like(score_ref)
            load_dec.wait()
            step_done = layer_step(0)
            send_on(0)
            release()
            release()
            sent = []

            @pl.when(s > 0)
            def _():
                more = []
                gather(up, 0, more, add_up)
                finish(more)

            @pl.when(s == 0)
            def _():
                more = []
                gather(up, 0, more, add_up, arrives=False)
                finish(more)

            step_done()
            weights_done()

        @pl.when(s >= 2)
        def _():
            step_done = layer_step(1)
            last = [last_z(dz) for dz in Z_FAR + (0,)] + [last_y(dy) for dy in Y_FAR + (0,)]
            for item in last[:7:2] + last[8:11] + last[1:8:2] + last[11:]:
                item.start()
            step_done()
            finish(last)

        @pl.when(s < 3)
        def _():
            out_gather()

        send_done()


def pick_kernel(pos_hbm, count_hbm, ids_hbm, act_hbm, score_hbm, grad_hbm, out_ref, grad_out_ref,
                pos_ref, count_ref, ids_ref, act_ref, score_ref, grad_ref, turned, picked, sem):
    pairs = ((score_hbm, score_ref), (grad_hbm, grad_ref), (pos_hbm, pos_ref), (count_hbm, count_ref),
             (ids_hbm, ids_ref), (act_hbm, act_ref))
    copies = [pltpu.make_async_copy(src, dst, sem.at[i]) for i, (src, dst) in enumerate(pairs)]
    for item in copies:
        item.start()
    copies[0].wait()
    turned[...] = score_ref[...].T
    copies[1].wait()
    grad_out_ref[0] = grad_ref[...].T.astype(BF16).reshape(TGT, SEQ, SL)
    for item in copies[2:]:
        item.wait()
    slots, width = ids_ref.shape[1], ids_ref.shape[2]
    for b in range(slots):
        at = pos_ref[0, b]
        for t in range(TGT):
            picked[t, b:b + 1, :] = turned[pl.ds(t * SEQ + at, 1), :]
    ids = ids_ref[0]
    live = lax.broadcasted_iota(jnp.int32, (slots, width), 0) < count_ref[0, 0]
    inner = ids % 128
    for t in range(TGT):
        low = jnp.take_along_axis(picked[t, :, :128], inner, axis=1, mode="promise_in_bounds")
        high = jnp.take_along_axis(picked[t, :, 128:], inner, axis=1, mode="promise_in_bounds")
        value = jnp.where(ids < 128, low, high) * act_ref[0]
        out_ref[0, t] = jnp.where(live, value, 0.0)


def body(
    target_ids, target_pos, target_gain, target_scale, encoder, post_gain, post_scale, out_proj, pattern,
    value_proj, pre_gain, pre_scale, decoder, block_ids, block_pos, block_act, block_count,
):
    vmem = pl.BlockSpec(memory_space=pltpu.VMEM)
    hbm = pl.BlockSpec(memory_space=pltpu.HBM)
    dma = pltpu.SemaphoreType.DMA
    shard = encoder.shape[0]
    features = decoder.shape[2]
    scores, grads = pl.pallas_call(
        main_kernel,
        out_shape=(
            jax.ShapeDtypeStruct((features, COLS), F32),
            jax.ShapeDtypeStruct((SL, COLS), F32),
        ),
        in_specs=[hbm] * 13,
        out_specs=(vmem, vmem),
        scratch_shapes=[
            pltpu.SMEM((2 * TGT,), jnp.int32),
            pltpu.SMEM((2 * TGT,), jnp.int32),
            pltpu.VMEM((D,), F32),
            pltpu.VMEM((1, SEQ), F32),
            pltpu.VMEM((1, D), F32),
            pltpu.VMEM((1, SEQ), F32),
            pltpu.VMEM((1, D), F32),
            pltpu.VMEM((1, SEQ), F32),
            pltpu.VMEM((1, 1, SEQ, SEQ), BF16),
            pltpu.VMEM((shard, D), BF16),
            pltpu.VMEM((HD, D), BF16),
            pltpu.VMEM((D, HD), BF16),
            pltpu.VMEM((2, features, D), BF16),
            pltpu.VMEM((8, D), F32),
            pltpu.VMEM((8, D), F32),
            pltpu.VMEM((8, D), F32),
            pltpu.VMEM((NY, 16, WIN), BF16),
            pltpu.VMEM((NY, 16, WIN), BF16),
            pltpu.VMEM((NZ, 16, WIN), BF16),
            pltpu.VMEM((NY, 16, WIN), BF16),
            pltpu.VMEM((16, WIN), BF16),
            pltpu.VMEM((FEATS, 16, COLS), BF16),
            pltpu.VMEM((FEATS, 16, COLS), BF16),
            pltpu.VMEM((FEATS, 8, SL), F32),
            pltpu.VMEM((FEATS, 1, SL), F32),
            pltpu.VMEM((2, NZ, HD, WIN), BF16),
            pltpu.VMEM((2, BLOCK, NZ * HD), BF16),
            pltpu.VMEM((2, COLS, COLS), BF16),
            pltpu.VMEM((2, BLOCK + 2 * PAD, COLS), BF16),
            pltpu.VMEM((2, NZ, HD, COLS), BF16),
            pltpu.VMEM((2, NZ, HD, COLS), BF16),
            pltpu.VMEM((2, NZ * HD, COLS), BF16),
            pltpu.VMEM((2, NY, SL, COLS), BF16),
            pltpu.VMEM((2, NY, SL, COLS), BF16),
            pltpu.VMEM((4, SL, COLS), BF16),
            pltpu.VMEM((D, COLS), BF16),
            pltpu.VMEM((D, COLS), BF16),
            dma((8,)),
            dma((9,)),
            dma((2,)),
            dma((3, NZ)),
            dma((3, NZ)),
            dma((FEATS,)),
            dma((FEATS,)),
            dma((2, NZ)),
            dma((2, NZ)),
            dma((2, 3)),
            dma((2, 3)),
            dma((2, NZ)),
            dma((2, NZ)),
            dma((3, NY)),
            dma((2, NY)),
            dma((8,)),
            dma((2, NZ)),
            dma((2, NZ)),
            dma((2, NZ)),
            dma((2, NZ)),
            dma((2, NY)),
            dma((2, NY)),
            dma((2, FEATS)),
            dma((2, FEATS)),
            dma((FEATS,)),
            dma((FEATS,)),
            pltpu.SemaphoreType.REGULAR,
        ],
        compiler_params=pltpu.CompilerParams(
            collective_id=1, has_side_effects=True, vmem_limit_bytes=60 * 1024 * 1024
        ),
        name="chain",
    )(
        target_ids, target_pos, target_gain, target_scale.reshape(1, SEQ), post_gain, post_scale,
        pre_gain, pre_scale, pattern, encoder, out_proj, value_proj, decoder,
    )
    slots, width = block_ids.shape[1], block_ids.shape[2]
    return pl.pallas_call(
        pick_kernel,
        out_shape=(
            jax.ShapeDtypeStruct((1, TGT, slots, width), F32),
            jax.ShapeDtypeStruct((1, TGT, SEQ, SL), BF16),
        ),
        in_specs=[hbm] * 6,
        out_specs=(vmem, vmem),
        scratch_shapes=[
            pltpu.SMEM((1, slots), jnp.int32),
            pltpu.SMEM((1, 1), jnp.int32),
            pltpu.VMEM((1, slots, width), jnp.int32),
            pltpu.VMEM((1, slots, width), F32),
            pltpu.VMEM((features, COLS), F32),
            pltpu.VMEM((SL, COLS), F32),
            pltpu.VMEM((COLS, features), F32),
            pltpu.VMEM((TGT, slots, features), F32),
            dma((6,)),
        ],
        name="pick",
    )(block_pos, block_count, block_ids, block_act, scores, grads)


def solution(mesh):
    in_specs = (
        P(),
        P(),
        P(),
        P(),
        P(("feat", "row"), None),
        P("section", None),
        P("section", None),
        P("section", "feat", None, None),
        P("section", "feat", None, None),
        P("section", "feat", None, None),
        P("section", None),
        P("section", None),
        P("section", None, "feat", None),
        P("section", "feat", None),
        P("section", "feat"),
        P("section", "feat", None),
        P("section", "feat"),
    )
    out_specs = (P("section", "row", "feat", None), P("section", "row", None, "feat"))
    return jax.shard_map(body, mesh=mesh, in_specs=in_specs, out_specs=out_specs, check_vma=False)
```
